256 devices in a mesh: circ: 32 (over z, y), span: 8 (over x, core).
Axes of the slice: x: 4, y: 4, z: 8, core: 2. Of those that a mesh axis runs over, the one named last changes fastest.
Arguments:
- increment: int32 [8], P('span'), may hold values from 1 to 4095, as said below
- partners: int32 [8, 4096], P('span', 'circ'), may hold values from 0 to 4095, as said below
- rotor_faces: float32 [90, 8, 4096], P(None, 'span', 'circ'), as said below
- stator_faces: float32 [90, 8, 4096], P(None, 'span', 'circ'), as said below
- solution: float32 [135, 8, 8192], P(None, 'span', 'circ'), may hold values from -6 to 6
- residual: float32 [135, 8, 8192], P(None, 'span', 'circ'), may hold values from -6 to 6
- inverse_blocks: bfloat16 [135, 135, 8, 8192], P(None, None, 'span', 'circ'), may hold values from -0.25 to 2
- halo_lists: int32 [2, 8, 8192], P(None, 'span', 'circ'), may hold values from 0 to 255, as said below
- lifting: float32 [135, 45], replicated, may hold values from -0.875 to 0.875
- traces: float32 [2, 45, 135], replicated, may hold values from -0.5 to 0.5
- couplings: float32 [2, 135, 45], replicated, may hold values from -0.875 to 0.875
Outputs:
- update: float32 [135, 8, 8192], P(None, 'span', 'circ')
- interface_flux: float32 [45, 8, 4096], P(None, 'span', 'circ')
The draws below stay inside these ranges and needn't reach their ends.
Inputs may be any that keep to these rules, and one draw needn't show every extreme that they name: No row's increment is a multiple of 128. `partners`: within each span row, the 128 rotor faces of an aligned block name each stator face of the same block exactly once. `halo_lists`: within each aligned block of 256 elements of a row, each list names each position 0 to 255 exactly once. `rotor_faces`: density and pressure are positive at every face point. `stator_faces`: density and pressure are positive at every face point.
All inputs are finite; a program needn't handle non-finite values.
Results may differ from the reference program's by a relative error of at most 0.0003.
Values sent between devices are 32-bit elements; how exact they have to be, the bound alone decides.
A program may use at most 64 MiB of HBM per device.

```python
import math
import jax
import jax.numpy as jnp
from jax import lax

FACE_DEV = 128
BLOCK = 135
FACE_VALUES = 45
SPANS = 8
NFC = 4096
ROW_ELEMS = 8192


GAS_GAMMA = 1.4


def face_states(key, velocity):
    subkeys = jax.random.split(key, 3)
    grid_shape = velocity.shape[1:]
    density = jnp.exp(jax.random.uniform(subkeys[0], grid_shape, jnp.float32, math.log(0.7), math.log(1.4)))
    pressure = jnp.exp(jax.random.uniform(subkeys[1], grid_shape, jnp.float32, math.log(0.6), math.log(1.4)))
    momentum = density[None] * velocity
    energy = pressure / (GAS_GAMMA - 1.0) + 0.5 * density * (velocity[0] * velocity[0] + velocity[1] * velocity[1] + velocity[2] * velocity[2])
    values = jnp.concatenate([density[None], momentum, energy[None]], axis=0).reshape(45, SPANS, NFC)
    slopes = jax.random.normal(subkeys[2], (45, SPANS, NFC), jnp.float32)
    return jnp.concatenate([values, slopes], axis=0)


def draw_rotor_faces(key, part):
    key = jax.random.fold_in(key, 11)
    velocity_key = jax.random.fold_in(key, 1)
    velocity = jnp.clip(0.3 * jax.random.normal(velocity_key, (3, 9, SPANS, NFC), jnp.float32), -0.9, 0.9)
    return face_states(key, velocity)


def draw_stator_faces(key, part):
    key = jax.random.fold_in(key, 12)
    velocity_key = jax.random.fold_in(key, 1)
    velocity = jnp.clip(0.3 * jax.random.normal(velocity_key, (3, 9, SPANS, NFC), jnp.float32), -0.9, 0.9)
    return face_states(key, velocity)


def draw_increment(key, part):
    key = jax.random.fold_in(key, 41)
    subkeys = jax.random.split(key, 3)
    blocks = NFC // FACE_DEV
    steps_drawn = jax.random.randint(subkeys[0], (SPANS,), 0, blocks)
    order = jax.random.permutation(subkeys[1], SPANS)
    leftover = jax.random.randint(subkeys[2], (SPANS,), 1, FACE_DEV)
    steps_drawn = jnp.where(order == 0, 0, jnp.where(order == 1, blocks - 1, jnp.where(order == 2, blocks // 2, steps_drawn)))
    leftover = jnp.where(order == 0, 1, jnp.where(order == 1, FACE_DEV - 1, leftover))
    return (steps_drawn * FACE_DEV + leftover).astype(jnp.int32)


def draw_partners(key, part):
    key = jax.random.fold_in(key, 21)
    blocks = NFC // FACE_DEV
    block_keys = jax.random.split(key, SPANS * blocks)
    orders = jax.vmap(lambda one_key: jax.random.permutation(one_key, FACE_DEV))(block_keys)
    starts = jnp.arange(SPANS * blocks, dtype=jnp.int32) % blocks * FACE_DEV
    return (orders.astype(jnp.int32) + starts[:, None]).reshape(SPANS, NFC)


def draw_halo_lists(key, part):
    key = jax.random.fold_in(key, 22)
    blocks = NFC // FACE_DEV
    block_keys = jax.random.split(key, 2 * SPANS * blocks)
    orders = jax.vmap(lambda one_key: jax.random.permutation(one_key, 2 * FACE_DEV))(block_keys)
    return orders.astype(jnp.int32).reshape(2, SPANS, 2 * NFC)


def draw_inverse_blocks(key, part):
    key = jax.random.fold_in(key, 31)
    subkeys = jax.random.split(key, 2)
    spread = jnp.clip(0.04 * jax.random.normal(subkeys[0], (135, 135, SPANS, ROW_ELEMS), jnp.float32), -0.2, 0.2)
    diagonal = jnp.exp(jax.random.uniform(subkeys[1], (135, SPANS, ROW_ELEMS), jnp.float32, math.log(0.5), math.log(2.0)))
    marker = jnp.eye(135, dtype=bool)[:, :, None, None]
    return jnp.where(marker, diagonal[None], spread).astype(jnp.bfloat16)


def levels(stream_key, extent, shards, low, largest):
    factor_of, own = 1.0, jax.random.fold_in(stream_key, 6)
    for axis_at, shards_of in shards:
        draws = jnp.exp(jax.random.uniform(jax.random.fold_in(own, axis_at), (shards_of,), jnp.float32, low / len(shards), largest / len(shards)))
        factor_of = factor_of * jnp.repeat(draws, extent[axis_at] // shards_of).reshape([-1 if axis == axis_at else 1 for axis in range(len(extent))])
    return factor_of


def gaussian(key, dims, scale, most, cuts=(), held_as=jnp.bfloat16):
    factor_of = levels(key, dims, cuts, -0.22, 0.18) if cuts else 1.0
    drawn = jax.random.normal(key, dims, jnp.float32) * scale * factor_of
    return jnp.minimum(jnp.maximum(drawn, -most), most).astype(held_as)


def setup_inputs(seed: int = 0) -> dict:
    key_list = jax.random.split(jax.random.key(seed), 12)
    return {
        "increment": draw_increment(jax.random.fold_in(key_list[11], 71), 0),
        "partners": draw_partners(jax.random.fold_in(key_list[11], 71), 0),
        "rotor_faces": draw_rotor_faces(jax.random.fold_in(key_list[11], 71), 0),
        "stator_faces": draw_stator_faces(jax.random.fold_in(key_list[11], 71), 0),
        "solution": gaussian(key_list[4], (BLOCK, SPANS, ROW_ELEMS), 1.0, 6.0, ((1, 8), (2, 32)), jnp.float32),
        "residual": gaussian(key_list[5], (BLOCK, SPANS, ROW_ELEMS), 1.0, 6.0, ((1, 8), (2, 32)), jnp.float32),
        "inverse_blocks": draw_inverse_blocks(jax.random.fold_in(key_list[11], 71), 0),
        "halo_lists": draw_halo_lists(jax.random.fold_in(key_list[11], 71), 0),
        "lifting": gaussian(key_list[8], (BLOCK, FACE_VALUES), FACE_VALUES ** -0.5, 0.875, (), jnp.float32),
        "traces": gaussian(key_list[9], (2, FACE_VALUES, BLOCK), BLOCK ** -0.5, 0.5, (), jnp.float32),
        "couplings": gaussian(key_list[10], (2, BLOCK, FACE_VALUES), FACE_VALUES ** -0.5, 0.875, (), jnp.float32),
    }


GAMMA = 1.4
VISCOSITY = 0.3

def euler_flux(state):
    density = state[0]
    mom_x = state[1]
    mom_y = state[2]
    mom_z = state[3]
    energy = state[4]
    vel_x = mom_x / density
    kinetic = 0.5 * (mom_x * mom_x + mom_y * mom_y + mom_z * mom_z) / density
    pressure = (GAMMA - 1.0) * (energy - kinetic)
    flux = jnp.stack([mom_x, mom_x * vel_x + pressure, mom_y * vel_x, mom_z * vel_x, (energy + pressure) * vel_x])
    wave_speed = jnp.abs(vel_x) + jnp.sqrt(GAMMA * pressure / density)
    return (flux, wave_speed)

def mortar(left_side, right_side):
    face_total = left_side.shape[-1]
    left_state = left_side[:45].reshape(5, 9, face_total)
    right_state = right_side[:45].reshape(5, 9, face_total)
    left_flux, left_speed = euler_flux(left_state)
    right_flux, right_speed = euler_flux(right_state)
    fastest = jnp.maximum(left_speed, right_speed)
    common = 0.5 * (left_flux + right_flux) - 0.5 * fastest * (right_state - left_state)
    return common.reshape(45, face_total) - 0.5 * VISCOSITY * (left_side[45:] + right_side[45:])

def reference(increment, partners, rotor_faces, stator_faces, solution, residual, inverse_blocks, halo_lists, lifting, traces, couplings):
    span_rows = partners.shape[0]
    cycle = partners.shape[1]
    highest = lax.Precision.HIGHEST
    target = ((partners + increment[:, None]) % cycle).astype(jnp.int32)
    row_index = jnp.arange(span_rows, dtype=jnp.int32)[:, None] * jnp.ones_like(target)
    arrived = jnp.zeros_like(rotor_faces).at[:, row_index, target].set(rotor_faces)
    flat = span_rows * cycle
    mortar_flux = mortar(arrived.reshape(90, flat), stator_faces.reshape(90, flat)).reshape(45, span_rows, cycle)
    rotor_flux = mortar_flux[:, row_index, target]
    blocks = cycle // FACE_DEV
    face_terms = jnp.concatenate([rotor_flux.reshape(45, span_rows, blocks, FACE_DEV), -mortar_flux.reshape(45, span_rows, blocks, FACE_DEV)], axis=3).reshape(45, span_rows, 2 * cycle)
    lifted = jnp.einsum('kf,fse->kse', lifting, face_terms, precision=highest)
    upper = jnp.einsum('fk,kse->fse', traces[0], solution, precision=highest)
    lower = jnp.einsum('fk,kse->fse', traces[1], solution, precision=highest)
    zero_row = jnp.zeros_like(upper[:, :1])
    from_below = jnp.concatenate([zero_row, upper[:, :-1]], axis=1)
    from_above = jnp.concatenate([lower[:, 1:], zero_row], axis=1)
    width = 2 * FACE_DEV
    base = jnp.arange(2 * cycle, dtype=jnp.int32) // width * width
    below_cols = (base[None, :] + halo_lists[0]).astype(jnp.int32)
    above_cols = (base[None, :] + halo_lists[1]).astype(jnp.int32)
    below_nbr = jnp.take_along_axis(from_below, below_cols[None], axis=2)
    above_nbr = jnp.take_along_axis(from_above, above_cols[None], axis=2)
    coupled = jnp.einsum('kf,fse->kse', couplings[0], below_nbr, precision=highest) + jnp.einsum('kf,fse->kse', couplings[1], above_nbr, precision=highest)
    rhs = residual - lifted - coupled
    pieces = []
    for row_number in range(span_rows):
        block_now = inverse_blocks[:, :, row_number].astype(jnp.float32)
        pieces.append(jnp.einsum('ije,je->ie', block_now, rhs[:, row_number], precision=highest))
    update = jnp.stack(pieces, axis=1)
    return (update, rotor_flux)
```

```python
import functools

import jax
import jax.numpy as jnp
from jax import lax
from jax.experimental import pallas as pl
from jax.experimental.pallas import tpu as pltpu
from jax.sharding import PartitionSpec as P

GAMMA = 1.4
VISCOSITY = 0.3
CIRC = 32
SPANS = 8
MESH = pl.DeviceIdType.MESH
NEAR = (1, -1, 2, -2)
MIDDLE = (4, -4)
FAR = (12, -12)
CHUNKS = 5


def two_parts(value):
    head = value.astype(jnp.bfloat16)
    return head, (value - head.astype(jnp.float32)).astype(jnp.bfloat16)


def mxu(left, right, dims=((1,), (0,))):
    return lax.dot_general(left, right, (dims, ((), ())), preferred_element_type=jnp.float32)


def dot3(left, right, dims=((1,), (0,))):
    left_head, left_tail = two_parts(left)
    right_head, right_tail = two_parts(right)
    small = mxu(left_head, right_tail, dims) + mxu(left_tail, right_head, dims)
    return mxu(left_head, right_head, dims) + small


def side_terms(ref):
    var = [ref[9 * v : 9 * v + 9, :] for v in range(5)]
    inverse = 1.0 / var[0]
    vel = var[1] * inverse
    kinetic = 0.5 * (var[1] * var[1] + var[2] * var[2] + var[3] * var[3]) * inverse
    pressure = (GAMMA - 1.0) * (var[4] - kinetic)
    flux = [var[1], var[1] * vel + pressure, var[2] * vel, var[3] * vel, (var[4] + pressure) * vel]
    terms = [
        0.5 * flux[v] - 0.5 * VISCOSITY * ref[45 + 9 * v : 54 + 9 * v, :] for v in range(5)
    ]
    return terms, jnp.abs(vel) + jnp.sqrt(GAMMA * pressure * inverse)


def kernel(
    inc_hbm, partners_hbm, rotor_hbm, stator_hbm, solution_hbm, residual_hbm, inverse_hbm, halo_hbm, lift_hbm,
    traces_hbm, couplings_hbm, update_hbm, flux_hbm,
    inc, partners, rotor, stator, state, residual, inverse, halo, lift, traces, couplings,
    one_hot, sorted_rotor, near_out, near_in, near_rotor, near_stator, middle_out, middle_in, middle_rotor,
    middle_stator, far_out, far_in, last_rotor, last_stator, trace_out, trace_in, lift_parts, lifted_blocks,
    rhs, base, own_terms, own_speed, face_terms, rotor_flux,
    load_sem, block_sem, send_sem, recv_sem, store_sem,
):
    me = lax.axis_index("circ")
    row = lax.axis_index("span")

    def at(circ_shift, span_shift=0):
        return (lax.rem(me + circ_shift + CIRC, CIRC), lax.rem(row + span_shift + SPANS, SPANS))

    barrier = pltpu.get_barrier_semaphore()
    for shift in NEAR + MIDDLE + FAR:
        pl.semaphore_signal(barrier, inc=1, device_id=at(shift), device_id_type=MESH)
    for shift in (1, -1):
        pl.semaphore_signal(barrier, inc=1, device_id=at(0, shift), device_id_type=MESH)

    pairs = [
        (partners_hbm, partners),
        (rotor_hbm.at[:, 0, :], rotor),
        (stator_hbm.at[:, 0, :], stator),
        (traces_hbm.at[:, 0, :], traces.at[0]),
        (traces_hbm.at[:, 1, :], traces.at[1]),
        (solution_hbm.at[:, 0, :], state),
        (lift_hbm, lift),
        (couplings_hbm.at[:, 0, :], couplings.at[0]),
        (couplings_hbm.at[:, 1, :], couplings.at[1]),
        (halo_hbm.at[:, 0, :], halo),
        (residual_hbm.at[:, 0, :], residual),
        (inc_hbm, inc),
    ]
    loads = [pltpu.make_async_copy(src, dst, load_sem.at[k]) for k, (src, dst) in enumerate(pairs)]
    for load in loads:
        load.start()
    rows = 135 // CHUNKS

    def block(k):
        part = pl.ds(rows * k, rows)
        return pltpu.make_async_copy(inverse_hbm.at[part], inverse.at[part], block_sem.at[k])

    for k in range(CHUNKS):
        block(k).start()

    loads[11].wait()
    increment = jnp.broadcast_to(inc[...], (1, 128))
    remainder = jnp.bitwise_and(increment, 127)
    whole = jnp.right_shift(increment, 7)
    lane = lax.broadcasted_iota(jnp.int32, (1, 128), 1)
    steps = whole + jnp.where(lane < remainder, 1, 0)
    digit_near = jnp.bitwise_and(steps + 1, 3) - 1
    quarter = jnp.bitwise_and(jnp.right_shift(steps - digit_near, 2), 7)

    def among(*values):
        hit = quarter == values[0]
        for value in values[1:]:
            hit = jnp.logical_or(hit, quarter == value)
        return jnp.where(hit, 1, 0)

    digit_middle = among(1, 4, 6) - among(2, 7)
    digit_far = among(2, 3, 4) - among(5, 6)

    def copies(first, shifts, sources, landing, span=False):
        made = []
        for k, shift in enumerate(shifts):
            made.append(
                pltpu.make_async_remote_copy(
                    src_ref=sources[k],
                    dst_ref=landing.at[k],
                    send_sem=send_sem.at[first + k],
                    recv_sem=recv_sem.at[first + k],
                    device_id=at(0, shift) if span else at(shift),
                    device_id_type=MESH,
                )
            )
        return made

    def spread(value):
        return jnp.broadcast_to(value, (90, 128))

    loads[0].wait()
    slot = jnp.bitwise_and(partners[...] + remainder, 127)
    sublane = lax.broadcasted_iota(jnp.int32, (128, 128), 0)
    one_hot[...] = jnp.where(sublane == jnp.broadcast_to(slot, (128, 128)), 1.0, 0.0).astype(jnp.bfloat16)
    loads[1].wait()
    faces = rotor[...]
    head, tail = two_parts(faces)
    rest = (faces - head.astype(jnp.float32) - tail.astype(jnp.float32)).astype(jnp.bfloat16)
    turn = one_hot[...]
    across = ((1,), (1,))
    sorted_rotor[...] = mxu(head, turn, across) + (mxu(tail, turn, across) + mxu(rest, turn, across))
    loads[2].wait()

    digit = spread(digit_near)
    near_out[0] = jnp.where(digit == 1, sorted_rotor[...], stator[...])
    near_out[1] = jnp.where(digit == -1, sorted_rotor[...], stator[...])
    near = copies(0, NEAR, [near_out.at[0], near_out.at[1], sorted_rotor, stator], near_in)
    pl.semaphore_wait(barrier, 10)
    for copy in near:
        copy.start()

    for k in range(3, 6):
        loads[k].wait()
    for k in range(2):
        trace_out[k] = dot3(traces[k], state[...])
    spans = copies(8, (1, -1), [trace_out.at[0], trace_out.at[1]], trace_in, span=True)
    for copy in spans:
        copy.start()

    def local_work():
        for k in range(6, 11):
            loads[k].wait()
        head, tail = two_parts(lift[...])
        lift_parts[...] = jnp.zeros((96, 135), jnp.bfloat16)
        lift_parts[0:45, :] = head
        lift_parts[48:93, :] = tail
        factor = lift_parts[...]

        def lift_rows(k, carry):
            block(k).wait()
            for i in range(rows):
                both = mxu(factor, inverse[rows * k + i])
                lifted_blocks[rows * k + i] = both[:48] + both[48:]
            return carry

        lax.fori_loop(0, CHUNKS, lift_rows, 0)
        for copy in spans:
            copy.wait_recv()
        position = lax.broadcasted_iota(jnp.int32, (256, 256), 0)
        total = residual[...]
        for k in range(2):
            edge = 0 if k == 0 else SPANS - 1
            arrived = trace_in[k] * jnp.where(row == edge, 0.0, 1.0)
            wanted = jnp.broadcast_to(halo[pl.ds(k, 1), :], (256, 256))
            pick = jnp.where(position == wanted, 1.0, 0.0).astype(jnp.bfloat16)
            head, tail = two_parts(arrived)
            total = total - dot3(couplings[k], mxu(head, pick) + mxu(tail, pick), ((0,), (0,)))
        rhs[...] = total

        def base_row(i):
            return jnp.sum(inverse[i].astype(jnp.float32) * rhs[...], axis=0, keepdims=True)

        def base_eight(k, carry):
            first = pl.multiple_of(8 * k, 8)
            base[pl.ds(first, 8), :] = jnp.concatenate([base_row(first + i) for i in range(8)], axis=0)
            return carry

        lax.fori_loop(0, 16, base_eight, 0)
        base[128:135, :] = jnp.concatenate([base_row(128 + i) for i in range(7)], axis=0)

    early = me < CIRC // 2

    @pl.when(early)
    def _():
        local_work()

    def merge(digit, plus, minus, rotor_ref, stator_ref, rotor_to, stator_to, two=None):
        digit = spread(digit)
        rotor_new = jnp.where(digit == 0, rotor_ref[...], jnp.where(digit == 1, plus[...], minus[...]))
        stator_new = jnp.where(digit == 0, stator_ref[...], jnp.where(digit == 1, minus[...], plus[...]))
        if two is not None:
            rotor_new = jnp.where(digit == 2, two[0][...], rotor_new)
            stator_new = jnp.where(digit == 2, two[1][...], stator_new)
        rotor_to[...] = rotor_new
        stator_to[...] = stator_new
        return rotor_new, stator_new

    for copy in near:
        copy.wait_recv()
    moved, met = merge(
        digit_near, near_in.at[0], near_in.at[1], sorted_rotor, stator, near_rotor, near_stator,
        (near_in.at[2], near_in.at[3]),
    )
    digit = spread(digit_middle)
    middle_out[0] = jnp.where(digit == 1, moved, met)
    middle_out[1] = jnp.where(digit == -1, moved, met)
    middle = copies(4, MIDDLE, [middle_out.at[0], middle_out.at[1]], middle_in)
    for copy in middle:
        copy.start()

    for copy in middle:
        copy.wait_recv()
    moved, met = merge(
        digit_middle, middle_in.at[0], middle_in.at[1], near_rotor, near_stator, middle_rotor, middle_stator
    )
    digit = spread(digit_far)
    far_out[0] = jnp.where(digit == 1, moved, met)
    far_out[1] = jnp.where(digit == -1, moved, met)
    far = copies(6, FAR, [far_out.at[0], far_out.at[1]], far_in)
    for copy in far:
        copy.start()

    @pl.when(jnp.logical_not(early))
    def _():
        local_work()

    for k, ref in enumerate((sorted_rotor, stator)):
        terms, speed = side_terms(ref)
        for v in range(5):
            own_terms[k, 9 * v : 9 * v + 9, :] = terms[v]
        own_speed[k] = speed

    for copy in far:
        copy.wait_recv()
    merge(digit_far, far_in.at[0], far_in.at[1], middle_rotor, middle_stator, last_rotor, last_stator)

    for k, (left, right) in enumerate(((sorted_rotor, last_stator), (last_rotor, stator))):
        terms, speed = side_terms(last_stator if k == 0 else last_rotor)
        fastest = 0.5 * jnp.maximum(speed, own_speed[k])
        for v in range(5):
            part = pl.ds(9 * v, 9)
            face_terms[k, part, :] = (
                own_terms[k, part, :] + terms[v] - fastest * (right[part, :] - left[part, :])
            )
    head, tail = two_parts(face_terms[0])
    turn = one_hot[...]
    rotor_flux[...] = mxu(head, turn) + mxu(tail, turn)
    store_flux = pltpu.make_async_copy(rotor_flux, flux_hbm.at[:, 0, :], store_sem.at[0])
    store_flux.start()
    terms = jnp.concatenate([-rotor_flux[...], face_terms[1]], axis=1)

    def finish(part):
        weighted = lifted_blocks[part, 0:45, :] * terms[None]
        base[part, :] += jnp.sum(weighted, axis=1)

    def finish_eight(k, carry):
        finish(pl.ds(pl.multiple_of(8 * k, 8), 8))
        return carry

    lax.fori_loop(0, 16, finish_eight, 0)
    finish(pl.ds(128, 7))
    store = pltpu.make_async_copy(base, update_hbm.at[:, 0, :], store_sem.at[1])
    store.start()
    for copy in near + middle + far + spans:
        copy.wait_send()
    store_flux.wait()
    store.wait()


def shards(
    increment,
    partners,
    rotor_faces,
    stator_faces,
    solution,
    residual,
    inverse_blocks,
    halo_lists,
    lifting,
    traces,
    couplings,
):
    def vmem(*shape, dtype=jnp.float32):
        return pltpu.VMEM(shape, dtype)

    face = (90, 128)
    anywhere = pl.BlockSpec(memory_space=pltpu.HBM)
    return pl.pallas_call(
        kernel,
        out_shape=(
            jax.ShapeDtypeStruct((135, 1, 256), jnp.float32),
            jax.ShapeDtypeStruct((45, 1, 128), jnp.float32),
        ),
        in_specs=[anywhere] * 11,
        out_specs=(anywhere, anywhere),
        scratch_shapes=[
            vmem(1, 1, dtype=jnp.int32),
            vmem(1, 128, dtype=jnp.int32),
            vmem(*face),
            vmem(*face),
            vmem(135, 256),
            vmem(135, 256),
            vmem(135, 135, 256, dtype=jnp.bfloat16),
            vmem(2, 256, dtype=jnp.int32),
            vmem(45, 135),
            vmem(2, 45, 135),
            vmem(2, 45, 135),
            vmem(128, 128, dtype=jnp.bfloat16),
            vmem(*face),
            vmem(2, *face),
            vmem(4, *face),
            vmem(*face),
            vmem(*face),
            vmem(2, *face),
            vmem(2, *face),
            vmem(*face),
            vmem(*face),
            vmem(2, *face),
            vmem(2, *face),
            vmem(*face),
            vmem(*face),
            vmem(2, 45, 256),
            vmem(2, 45, 256),
            vmem(96, 135, dtype=jnp.bfloat16),
            vmem(135, 48, 256),
            vmem(135, 256),
            vmem(135, 256),
            vmem(2, 45, 128),
            vmem(2, 9, 128),
            vmem(2, 45, 128),
            vmem(45, 128),
            pltpu.SemaphoreType.DMA((12,)),
            pltpu.SemaphoreType.DMA((CHUNKS,)),
            pltpu.SemaphoreType.DMA((10,)),
            pltpu.SemaphoreType.DMA((10,)),
            pltpu.SemaphoreType.DMA((2,)),
        ],
        compiler_params=pltpu.CompilerParams(
            collective_id=0, has_side_effects=True, vmem_limit_bytes=60 * 1024 * 1024
        ),
    )(
        increment.reshape(1, 1),
        partners,
        rotor_faces,
        stator_faces,
        solution,
        residual,
        inverse_blocks.reshape(135, 135, 256),
        halo_lists,
        lifting.T,
        traces.transpose(1, 0, 2),
        couplings.transpose(2, 0, 1),
    )


def solution(mesh):
    placed = (
        P("span"),
        P("span", "circ"),
        P(None, "span", "circ"),
        P(None, "span", "circ"),
        P(None, "span", "circ"),
        P(None, "span", "circ"),
        P(None, None, "span", "circ"),
        P(None, "span", "circ"),
        P(),
        P(),
        P(),
    )
    return jax.shard_map(
        shards,
        mesh=mesh,
        in_specs=placed,
        out_specs=(P(None, "span", "circ"), P(None, "span", "circ")),
        check_vma=False,
    )
```

```python
import functools

import jax
import jax.numpy as jnp
from jax import lax
from jax.experimental import pallas as pl
from jax.experimental.pallas import tpu as pltpu
from jax.sharding import PartitionSpec as P

GAMMA = 1.4
VISCOSITY = 0.3
CIRC = 32
SPANS = 8
MESH = pl.DeviceIdType.MESH
STEPS = {"near": (1, -1, 2, -2), "middle": (4, -4), "far": (12, -12)}
KINDS = ("near", "middle", "far")
ORDERS = (("far", "middle", "near"), ("near", "middle", "far"))
STAY = 4
DIGITS = 6
PER_STAGE = 7
CHUNKS = 5
KA = 50 * 1024 * 1024
KB = 4 * 1024 * 1024


def two_parts(value):
    head = value.astype(jnp.bfloat16)
    return head, (value - head.astype(jnp.float32)).astype(jnp.bfloat16)


def mxu(left, right, dims=((1,), (0,))):
    return lax.dot_general(left, right, (dims, ((), ())), preferred_element_type=jnp.float32)


def dot3(left, right, dims=((1,), (0,))):
    left_head, left_tail = two_parts(left)
    right_head, right_tail = two_parts(right)
    small = mxu(left_head, right_tail, dims) + mxu(left_tail, right_head, dims)
    return mxu(left_head, right_head, dims) + small


def side_terms(ref):
    var = [ref[9 * v : 9 * v + 9, :] for v in range(5)]
    inverse = 1.0 / var[0]
    vel = var[1] * inverse
    kinetic = 0.5 * (var[1] * var[1] + var[2] * var[2] + var[3] * var[3]) * inverse
    pressure = (GAMMA - 1.0) * (var[4] - kinetic)
    flux = [var[1], var[1] * vel + pressure, var[2] * vel, var[3] * vel, (var[4] + pressure) * vel]
    terms = [
        0.5 * flux[v] - 0.5 * VISCOSITY * ref[45 + 9 * v : 54 + 9 * v, :] for v in range(5)
    ]
    return terms, jnp.abs(vel) + jnp.sqrt(GAMMA * pressure * inverse)


def kernel(
    inc_hbm, partners_hbm, rotor_hbm, stator_hbm, solution_hbm, residual_hbm, inverse_hbm, halo_hbm, lift_hbm,
    traces_hbm, couplings_hbm, lifted_blocks, base, terms_ref, rotor_flux,
    inc, partners, rotor, stator, state, residual, inverse, halo, lift, traces, couplings,
    one_hot, sorted_rotor, own_digits, guest_digits, moving, last_rotor, last_stator,
    slots_out, slots_in, trace_out, trace_in, lift_parts, rhs, own_terms, own_speed, face_terms,
    load_sem, block_sem, send_sem, recv_sem,
):
    me = lax.axis_index("circ")
    row = lax.axis_index("span")

    def at(circ_shift, span_shift=0):
        return (lax.rem(me + circ_shift + CIRC, CIRC), lax.rem(row + span_shift + SPANS, SPANS))

    even = lax.rem(row, 2) == 0
    odd = jnp.logical_not(even)
    first_even, last_even = STEPS[ORDERS[0][0]], STEPS[ORDERS[0][2]]
    every = STEPS["far"] + STEPS["middle"] + STEPS["near"]
    barrier = pltpu.get_barrier_semaphore()

    def greet(circ_shift, span_shift):
        pl.semaphore_signal(barrier, inc=1, device_id=at(circ_shift, span_shift), device_id_type=MESH)

    @pl.when(even)
    def _():
        for shift in last_even:
            greet(shift, 1)
        greet(0, 1)
        greet(0, -1)

    @pl.when(odd)
    def _():
        for shift in every:
            greet(shift, 0)
        for shift in first_even:
            greet(shift, -1)
        greet(0, -1)
        greet(0, 1)

    pairs = [
        (partners_hbm, partners),
        (inc_hbm, inc),
        (rotor_hbm.at[:, 0, :], rotor),
        (stator_hbm.at[:, 0, :], stator),
        (traces_hbm.at[:, 0, :], traces.at[0]),
        (traces_hbm.at[:, 1, :], traces.at[1]),
        (solution_hbm.at[:, 0, :], state),
        (lift_hbm, lift),
        (couplings_hbm.at[:, 0, :], couplings.at[0]),
        (couplings_hbm.at[:, 1, :], couplings.at[1]),
        (halo_hbm.at[:, 0, :], halo),
        (residual_hbm.at[:, 0, :], residual),
    ]
    loads = [pltpu.make_async_copy(src, dst, load_sem.at[k]) for k, (src, dst) in enumerate(pairs)]
    for load in loads[:4]:
        load.start()
    rows = 135 // CHUNKS

    def block(k):
        part = pl.ds(rows * k, rows)
        return pltpu.make_async_copy(inverse_hbm.at[part], inverse.at[part], block_sem.at[k])

    def load_rest():
        for load in loads[4:]:
            load.start()
        for k in range(CHUNKS):
            block(k).start()

    early = me < CIRC // 2
    late = jnp.logical_not(early)

    @pl.when(early)
    def _():
        load_rest()

    loads[0].wait()
    loads[1].wait()
    increment = jnp.broadcast_to(inc[...], (1, 128))
    remainder = jnp.bitwise_and(increment, 127)
    whole = jnp.right_shift(increment, 7)
    lane = lax.broadcasted_iota(jnp.int32, (1, 128), 1)
    steps = whole + jnp.where(lane < remainder, 1, 0)
    near_digit = jnp.bitwise_and(steps + 1, 3) - 1
    quarter = jnp.bitwise_and(jnp.right_shift(steps - near_digit, 2), 7)

    def among(*values):
        hit = quarter == values[0]
        for value in values[1:]:
            hit = jnp.logical_or(hit, quarter == value)
        return jnp.where(hit, 1, 0)

    middle_digit = among(1, 4, 6) - among(2, 7)
    far_digit = among(2, 3, 4) - among(5, 6)

    own_digits[...] = jnp.zeros((8, 128), jnp.float32)
    for k, value in enumerate((near_digit, middle_digit, far_digit)):
        own_digits[k : k + 1, :] = value.astype(jnp.float32)

    def slot_copy(group, stage, k, device, source):
        index = (3 * group + stage) * PER_STAGE + k
        return pltpu.make_async_remote_copy(
            src_ref=source,
            dst_ref=guest_digits if k == DIGITS else slots_in.at[6 * (3 * group + stage) + k],
            send_sem=send_sem.at[index],
            recv_sem=recv_sem.at[index],
            device_id=device,
            device_id_type=MESH,
        )

    def stage_copies(group, stage, rotor_ref, stator_ref):
        change = 0 if group == 1 or stage == 1 else 1 if stage == 0 else -1
        out = 2 * (3 * group + stage)
        sources = [slots_out.at[out], slots_out.at[out + 1], rotor_ref, stator_ref]
        made = [
            slot_copy(group, stage, k, at(shift, change), sources[k])
            for k, shift in enumerate(STEPS[ORDERS[group][stage]])
        ]
        if change:
            made.append(slot_copy(group, stage, STAY, at(0, change), rotor_ref))
            made.append(slot_copy(group, stage, STAY + 1, at(0, change), stator_ref))
        if change == 1:
            made.append(slot_copy(group, stage, DIGITS, at(0, change), own_digits))
        return made

    def digit_of(group, stage, digits):
        kind = KINDS.index(ORDERS[group][stage])
        return jnp.broadcast_to(digits[kind : kind + 1, :], (90, 128))

    def prepare(group, stage, digits, rotor_now, stator_now):
        digit = digit_of(group, stage, digits)
        out = 2 * (3 * group + stage)
        slots_out[out] = jnp.where(digit == 1.0, rotor_now, stator_now)
        slots_out[out + 1] = jnp.where(digit == -1.0, rotor_now, stator_now)

    def start(copies):
        for copy in copies:
            copy.start()

    def land(group, stage, copies, digits, rotor_ref, stator_ref, rotor_to, stator_to):
        for copy in copies:
            copy.wait_recv()
        digit = digit_of(group, stage, digits)
        slot = 6 * (3 * group + stage)
        plus, minus = slots_in[slot], slots_in[slot + 1]
        if group == 0 and stage != 1:
            rotor_ref, stator_ref = slots_in.at[slot + STAY], slots_in.at[slot + STAY + 1]
        rotor_new = jnp.where(digit == 0.0, rotor_ref[...], jnp.where(digit == 1.0, plus, minus))
        stator_new = jnp.where(digit == 0.0, stator_ref[...], jnp.where(digit == 1.0, minus, plus))
        if ORDERS[group][stage] == "near":
            rotor_new = jnp.where(digit == 2.0, slots_in[slot + 2], rotor_new)
            stator_new = jnp.where(digit == 2.0, slots_in[slot + 3], stator_new)
        rotor_to[...] = rotor_new
        stator_to[...] = stator_new
        return rotor_new, stator_new

    slot = jnp.bitwise_and(partners[...] + remainder, 127)
    sublane = lax.broadcasted_iota(jnp.int32, (128, 128), 0)
    one_hot[...] = jnp.where(sublane == jnp.broadcast_to(slot, (128, 128)), 1.0, 0.0).astype(jnp.bfloat16)
    turn = one_hot[...]
    across = ((1,), (1,))
    loads[2].wait()
    faces = rotor[...]
    head, tail = two_parts(faces)
    rest = (faces - head.astype(jnp.float32) - tail.astype(jnp.float32)).astype(jnp.bfloat16)
    in_order = mxu(head, turn, across) + (mxu(tail, turn, across) + mxu(rest, turn, across))
    sorted_rotor[...] = in_order
    loads[3].wait()
    for group, mine in enumerate((even, odd)):

        @pl.when(mine)
        def _(group=group):
            prepare(group, 0, own_digits, sorted_rotor[...], stator[...])

    spans = [
        pltpu.make_async_remote_copy(
            src_ref=trace_out.at[k],
            dst_ref=trace_in.at[k],
            send_sem=send_sem.at[6 * PER_STAGE + k],
            recv_sem=recv_sem.at[6 * PER_STAGE + k],
            device_id=at(0, shift),
            device_id_type=MESH,
        )
        for k, shift in enumerate((1, -1))
    ]

    def make_traces():
        for k in range(4, 7):
            loads[k].wait()
        for k in range(2):
            trace_out[k] = dot3(traces[k], state[...])

    def lift_blocks():
        loads[7].wait()
        head, tail = two_parts(lift[...])
        lift_parts[...] = jnp.zeros((96, 135), jnp.bfloat16)
        lift_parts[0:45, :] = head
        lift_parts[48:93, :] = tail
        factor = lift_parts[...]

        def lift_rows(k, carry):
            block(k).wait()
            for i in range(rows):
                both = mxu(factor, inverse[rows * k + i])
                lifted_blocks[rows * k + i] = both[:48] + both[48:]
            return carry

        lax.fori_loop(0, CHUNKS, lift_rows, 0)

    def multiply_base():
        for k in range(8, 12):
            loads[k].wait()
        for copy in spans:
            copy.wait_recv()
        position = lax.broadcasted_iota(jnp.int32, (256, 256), 0)
        total = residual[...]
        for k in range(2):
            edge = 0 if k == 0 else SPANS - 1
            arrived = trace_in[k] * jnp.where(row == edge, 0.0, 1.0)
            wanted = jnp.broadcast_to(halo[pl.ds(k, 1), :], (256, 256))
            pick = jnp.where(position == wanted, 1.0, 0.0).astype(jnp.bfloat16)
            head, tail = two_parts(arrived)
            total = total - dot3(couplings[k], mxu(head, pick) + mxu(tail, pick), ((0,), (0,)))
        rhs[...] = total

        def base_row(i):
            return jnp.sum(inverse[i].astype(jnp.float32) * rhs[...], axis=0, keepdims=True)

        def base_eight(k, carry):
            first = pl.multiple_of(8 * k, 8)
            base[pl.ds(first, 8), :] = jnp.concatenate([base_row(first + i) for i in range(8)], axis=0)
            return carry

        lax.fori_loop(0, 16, base_eight, 0)
        base[128:135, :] = jnp.concatenate([base_row(128 + i) for i in range(7)], axis=0)

    @pl.when(early)
    def _():
        make_traces()
        lift_blocks()

    @pl.when(even)
    def _():
        pl.semaphore_wait(barrier, len(first_even) + 2)
        start(stage_copies(0, 0, sorted_rotor, stator))

    @pl.when(odd)
    def _():
        pl.semaphore_wait(barrier, len(every) + len(last_even) + 2)
        start(stage_copies(1, 0, sorted_rotor, stator))

    @pl.when(late)
    def _():
        load_rest()
        make_traces()

    for copy in spans:
        copy.start()

    @pl.when(odd)
    def _():
        for stage in (1, 2):
            for group in (0, 1):
                digits = guest_digits if group == 0 else own_digits
                before = stage_copies(group, stage - 1, sorted_rotor, stator)
                if stage == 1:
                    rotor_ref, stator_ref = sorted_rotor, stator
                else:
                    rotor_ref, stator_ref = moving.at[2 * group], moving.at[2 * group + 1]
                to = 2 * group + (4 if stage == 2 else 0)
                moved, met = land(
                    group, stage - 1, before, digits, rotor_ref, stator_ref, moving.at[to], moving.at[to + 1]
                )
                prepare(group, stage, digits, moved, met)
                start(stage_copies(group, stage, moving.at[to], moving.at[to + 1]))

    @pl.when(late)
    def _():
        lift_blocks()

    multiply_base()

    for k, ref in enumerate((sorted_rotor, stator)):
        terms, speed = side_terms(ref)
        for v in range(5):
            own_terms[k, pl.ds(9 * v, 9), :] = terms[v]
        own_speed[k] = speed

    for group, mine in enumerate((even, odd)):

        @pl.when(mine)
        def _(group=group):
            arriving = stage_copies(group, 2, moving.at[6], moving.at[7])
            land(group, 2, arriving, own_digits, moving.at[6], moving.at[7], last_rotor, last_stator)

    for k, (left, right) in enumerate(((sorted_rotor, last_stator), (last_rotor, stator))):
        terms, speed = side_terms(last_stator if k == 0 else last_rotor)
        fastest = 0.5 * jnp.maximum(speed, own_speed[k])
        for v in range(5):
            part = pl.ds(9 * v, 9)
            face_terms[k, part, :] = (
                own_terms[k, part, :] + terms[v] - fastest * (right[part, :] - left[part, :])
            )
    head, tail = two_parts(face_terms[0])
    turn = one_hot[...]
    flux = mxu(head, turn) + mxu(tail, turn)
    rotor_flux[...] = flux
    terms_ref[:, 0:128] = -flux
    terms_ref[:, 128:256] = face_terms[1]
    for copy in spans:
        copy.wait_send()

    @pl.when(even)
    def _():
        for copy in stage_copies(0, 0, sorted_rotor, stator):
            copy.wait_send()

    @pl.when(odd)
    def _():
        for group, stage in ((1, 0), (0, 1), (1, 1), (0, 2), (1, 2)):
            to = 2 * group + (4 if stage == 2 else 0)
            for copy in stage_copies(group, stage, moving.at[to], moving.at[to + 1]):
                copy.wait_send()


def finish_kernel(lifted_blocks, base, terms_ref, rotor_flux, update_hbm, flux_hbm, update, store_sem):
    store_flux = pltpu.make_async_copy(rotor_flux, flux_hbm.at[:, 0, :], store_sem.at[0])
    store_flux.start()
    terms = terms_ref[...]

    def finish(part):
        weighted = lifted_blocks[part, 0:45, :] * terms[None]
        update[part, :] = base[part, :] + jnp.sum(weighted, axis=1)

    def finish_eight(k, carry):
        finish(pl.ds(pl.multiple_of(8 * k, 8), 8))
        return carry

    stores = []
    for k, (start, stop) in enumerate(((0, 64), (64, 128), (128, 135))):
        if stop == 135:
            finish(pl.ds(start, 7))
        else:
            lax.fori_loop(start // 8, stop // 8, finish_eight, 0)
        part = pl.ds(start, stop - start)
        store = pltpu.make_async_copy(update.at[part], update_hbm.at[part, 0, :], store_sem.at[1 + k])
        store.start()
        stores.append(store)
    store_flux.wait()
    for store in stores:
        store.wait()


def shards(
    increment,
    partners,
    rotor_faces,
    stator_faces,
    solution,
    residual,
    inverse_blocks,
    halo_lists,
    lifting,
    traces,
    couplings,
):
    def vmem(*shape, dtype=jnp.float32):
        return pltpu.VMEM(shape, dtype)

    face = (90, 128)
    anywhere = pl.BlockSpec(memory_space=pltpu.HBM)
    held = pl.pallas_call(
        kernel,
        out_shape=(
            vmem(135, 48, 256),
            vmem(135, 256),
            vmem(45, 256),
            vmem(45, 128),
        ),
        in_specs=[anywhere] * 11,
        out_specs=[pl.BlockSpec(memory_space=pltpu.VMEM)] * 4,
        scratch_shapes=[
            vmem(1, 1, dtype=jnp.int32),
            vmem(1, 128, dtype=jnp.int32),
            vmem(*face),
            vmem(*face),
            vmem(135, 256),
            vmem(135, 256),
            vmem(135, 135, 256, dtype=jnp.bfloat16),
            vmem(2, 256, dtype=jnp.int32),
            vmem(45, 135),
            vmem(2, 45, 135),
            vmem(2, 45, 135),
            vmem(128, 128, dtype=jnp.bfloat16),
            vmem(*face),
            vmem(8, 128),
            vmem(8, 128),
            vmem(8, *face),
            vmem(*face),
            vmem(*face),
            vmem(12, *face),
            vmem(36, *face),
            vmem(2, 45, 256),
            vmem(2, 45, 256),
            vmem(96, 135, dtype=jnp.bfloat16),
            vmem(135, 256),
            vmem(2, 45, 128),
            vmem(2, 9, 128),
            vmem(2, 45, 128),
            pltpu.SemaphoreType.DMA((12,)),
            pltpu.SemaphoreType.DMA((CHUNKS,)),
            pltpu.SemaphoreType.DMA((6 * PER_STAGE + 2,)),
            pltpu.SemaphoreType.DMA((6 * PER_STAGE + 2,)),
        ],
        compiler_params=pltpu.CompilerParams(
            collective_id=0, has_side_effects=True, vmem_limit_bytes=KA
        ),
    )(
        increment.reshape(1, 1),
        partners,
        rotor_faces,
        stator_faces,
        solution,
        residual,
        inverse_blocks.reshape(135, 135, 256),
        halo_lists,
        lifting.T,
        traces.transpose(1, 0, 2),
        couplings.transpose(2, 0, 1),
    )
    return pl.pallas_call(
        finish_kernel,
        out_shape=(
            jax.ShapeDtypeStruct((135, 1, 256), jnp.float32),
            jax.ShapeDtypeStruct((45, 1, 128), jnp.float32),
        ),
        in_specs=[pl.BlockSpec(memory_space=pltpu.VMEM)] * 4,
        out_specs=(anywhere, anywhere),
        scratch_shapes=[vmem(135, 256), pltpu.SemaphoreType.DMA((4,))],
        compiler_params=pltpu.CompilerParams(vmem_limit_bytes=KB),
    )(*held)


def solution(mesh):
    placed = (
        P("span"),
        P("span", "circ"),
        P(None, "span", "circ"),
        P(None, "span", "circ"),
        P(None, "span", "circ"),
        P(None, "span", "circ"),
        P(None, None, "span", "circ"),
        P(None, "span", "circ"),
        P(),
        P(),
        P(),
    )
    return jax.shard_map(
        shards,
        mesh=mesh,
        in_specs=placed,
        out_specs=(P(None, "span", "circ"), P(None, "span", "circ")),
        check_vma=False,
    )
```

```python
import functools

import jax
import jax.numpy as jnp
from jax import lax
from jax.experimental import pallas as pl
from jax.experimental.pallas import tpu as pltpu
from jax.sharding import PartitionSpec as P

GAMMA = 1.4
VISCOSITY = 0.3
CIRC = 32
SPANS = 8
MESH = pl.DeviceIdType.MESH
STEPS = {"near": (1, -1, 2, -2), "middle": (4, -4), "far": (12, -12)}
KINDS = ("near", "middle", "far")
ORDERS = (("middle", "far", "near"), ("near", "middle", "far"))
STAY = 4
DIGITS = 6
PER_STAGE = 7
CHUNKS = 5
KA = 50 * 1024 * 1024
KB = 4 * 1024 * 1024


def two_parts(value):
    head = value.astype(jnp.bfloat16)
    return head, (value - head.astype(jnp.float32)).astype(jnp.bfloat16)


def mxu(left, right, dims=((1,), (0,))):
    return lax.dot_general(left, right, (dims, ((), ())), preferred_element_type=jnp.float32)


def dot3(left, right, dims=((1,), (0,))):
    left_head, left_tail = two_parts(left)
    right_head, right_tail = two_parts(right)
    small = mxu(left_head, right_tail, dims) + mxu(left_tail, right_head, dims)
    return mxu(left_head, right_head, dims) + small


def side_terms(ref):
    var = [ref[9 * v : 9 * v + 9, :] for v in range(5)]
    inverse = 1.0 / var[0]
    vel = var[1] * inverse
    kinetic = 0.5 * (var[1] * var[1] + var[2] * var[2] + var[3] * var[3]) * inverse
    pressure = (GAMMA - 1.0) * (var[4] - kinetic)
    flux = [var[1], var[1] * vel + pressure, var[2] * vel, var[3] * vel, (var[4] + pressure) * vel]
    terms = [
        0.5 * flux[v] - 0.5 * VISCOSITY * ref[45 + 9 * v : 54 + 9 * v, :] for v in range(5)
    ]
    return terms, jnp.abs(vel) + jnp.sqrt(GAMMA * pressure * inverse)


def kernel(
    inc_hbm, partners_hbm, rotor_hbm, stator_hbm, solution_hbm, residual_hbm, inverse_hbm, halo_hbm, lift_hbm,
    traces_hbm, couplings_hbm, lifted_blocks, base, terms_ref, rotor_flux,
    inc, partners, rotor, stator, state, residual, inverse, halo, lift, traces, couplings,
    one_hot, sorted_rotor, own_digits, guest_digits, moving, last_rotor, last_stator,
    slots_out, slots_in, trace_out, trace_in, lift_parts, rhs, own_terms, own_speed, face_terms,
    load_sem, block_sem, send_sem, recv_sem,
):
    me = lax.axis_index("circ")
    row = lax.axis_index("span")

    def at(circ_shift, span_shift=0):
        return (lax.rem(me + circ_shift + CIRC, CIRC), lax.rem(row + span_shift + SPANS, SPANS))

    pairs = [
        (partners_hbm, partners),
        (inc_hbm, inc),
        (rotor_hbm.at[:, 0, :], rotor),
        (stator_hbm.at[:, 0, :], stator),
        (traces_hbm.at[:, 0, :], traces.at[0]),
        (traces_hbm.at[:, 1, :], traces.at[1]),
        (solution_hbm.at[:, 0, :], state),
        (lift_hbm, lift),
        (couplings_hbm.at[:, 0, :], couplings.at[0]),
        (couplings_hbm.at[:, 1, :], couplings.at[1]),
        (halo_hbm.at[:, 0, :], halo),
        (residual_hbm.at[:, 0, :], residual),
    ]
    loads = [pltpu.make_async_copy(src, dst, load_sem.at[k]) for k, (src, dst) in enumerate(pairs)]
    for load in loads[:4]:
        load.start()
    even = lax.rem(row, 2) == 0
    odd = jnp.logical_not(even)
    first_even, last_even = STEPS[ORDERS[0][0]], STEPS[ORDERS[0][2]]
    every = STEPS["far"] + STEPS["middle"] + STEPS["near"]
    barrier = pltpu.get_barrier_semaphore()

    def greet(circ_shift, span_shift):
        pl.semaphore_signal(barrier, inc=1, device_id=at(circ_shift, span_shift), device_id_type=MESH)

    @pl.when(even)
    def _():
        for shift in last_even:
            greet(shift, 1)
        greet(0, 1)
        greet(0, -1)

    @pl.when(odd)
    def _():
        for shift in first_even:
            greet(shift, -1)
        for shift in every:
            greet(shift, 0)
        greet(0, -1)
        greet(0, 1)

    rows = 135 // CHUNKS

    def block(k):
        part = pl.ds(rows * k, rows)
        return pltpu.make_async_copy(inverse_hbm.at[part], inverse.at[part], block_sem.at[k])

    def load_rest():
        for load in loads[4:]:
            load.start()
        for k in range(CHUNKS):
            block(k).start()

    early = me < 12
    late = jnp.logical_not(early)

    @pl.when(early)
    def _():
        load_rest()

    loads[0].wait()
    loads[1].wait()
    increment = jnp.broadcast_to(inc[...], (1, 128))
    remainder = jnp.bitwise_and(increment, 127)
    whole = jnp.right_shift(increment, 7)
    lane = lax.broadcasted_iota(jnp.int32, (1, 128), 1)
    steps = whole + jnp.where(lane < remainder, 1, 0)
    near_digit = jnp.bitwise_and(steps + 1, 3) - 1
    quarter = jnp.bitwise_and(jnp.right_shift(steps - near_digit, 2), 7)

    def among(*values):
        hit = quarter == values[0]
        for value in values[1:]:
            hit = jnp.logical_or(hit, quarter == value)
        return jnp.where(hit, 1, 0)

    middle_digit = among(1, 4, 6) - among(2, 7)
    far_digit = among(2, 3, 4) - among(5, 6)

    own_digits[...] = jnp.zeros((8, 128), jnp.float32)
    for k, value in enumerate((near_digit, middle_digit, far_digit)):
        own_digits[k : k + 1, :] = value.astype(jnp.float32)

    def slot_copy(group, stage, k, device, source):
        index = (3 * group + stage) * PER_STAGE + k
        return pltpu.make_async_remote_copy(
            src_ref=source,
            dst_ref=guest_digits if k == DIGITS else slots_in.at[6 * (3 * group + stage) + k],
            send_sem=send_sem.at[index],
            recv_sem=recv_sem.at[index],
            device_id=device,
            device_id_type=MESH,
        )

    def stage_copies(group, stage, rotor_ref, stator_ref):
        change = 0 if group == 1 or stage == 1 else 1 if stage == 0 else -1
        out = 2 * (3 * group + stage)
        sources = [slots_out.at[out], slots_out.at[out + 1], rotor_ref, stator_ref]
        made = [
            slot_copy(group, stage, k, at(shift, change), sources[k])
            for k, shift in enumerate(STEPS[ORDERS[group][stage]])
        ]
        if change:
            made.append(slot_copy(group, stage, STAY, at(0, change), rotor_ref))
            made.append(slot_copy(group, stage, STAY + 1, at(0, change), stator_ref))
        if change == 1:
            made.append(slot_copy(group, stage, DIGITS, at(0, change), own_digits))
        return made

    def digit_of(group, stage, digits):
        kind = KINDS.index(ORDERS[group][stage])
        return jnp.broadcast_to(digits[kind : kind + 1, :], (90, 128))

    def prepare(group, stage, digits, rotor_now, stator_now):
        digit = digit_of(group, stage, digits)
        out = 2 * (3 * group + stage)
        slots_out[out] = jnp.where(digit == 1.0, rotor_now, stator_now)
        slots_out[out + 1] = jnp.where(digit == -1.0, rotor_now, stator_now)

    def start(copies):
        for copy in copies:
            copy.start()

    def land(group, stage, copies, digits, rotor_ref, stator_ref, rotor_to, stator_to):
        for copy in copies:
            copy.wait_recv()
        digit = digit_of(group, stage, digits)
        slot = 6 * (3 * group + stage)
        plus, minus = slots_in[slot], slots_in[slot + 1]
        if group == 0 and stage != 1:
            rotor_ref, stator_ref = slots_in.at[slot + STAY], slots_in.at[slot + STAY + 1]
        rotor_new = jnp.where(digit == 0.0, rotor_ref[...], jnp.where(digit == 1.0, plus, minus))
        stator_new = jnp.where(digit == 0.0, stator_ref[...], jnp.where(digit == 1.0, minus, plus))
        if ORDERS[group][stage] == "near":
            rotor_new = jnp.where(digit == 2.0, slots_in[slot + 2], rotor_new)
            stator_new = jnp.where(digit == 2.0, slots_in[slot + 3], stator_new)
        rotor_to[...] = rotor_new
        stator_to[...] = stator_new
        return rotor_new, stator_new

    slot = jnp.bitwise_and(partners[...] + remainder, 127)
    sublane = lax.broadcasted_iota(jnp.int32, (128, 128), 0)
    one_hot[...] = jnp.where(sublane == jnp.broadcast_to(slot, (128, 128)), 1.0, 0.0).astype(jnp.bfloat16)
    turn = one_hot[...]
    across = ((1,), (1,))
    loads[2].wait()
    faces = rotor[...]
    head, tail = two_parts(faces)
    rest = (faces - head.astype(jnp.float32) - tail.astype(jnp.float32)).astype(jnp.bfloat16)
    in_order = mxu(head, turn, across) + (mxu(tail, turn, across) + mxu(rest, turn, across))
    sorted_rotor[...] = in_order
    loads[3].wait()
    for group, mine in enumerate((even, odd)):

        @pl.when(mine)
        def _(group=group):
            prepare(group, 0, own_digits, sorted_rotor[...], stator[...])

    spans = [
        pltpu.make_async_remote_copy(
            src_ref=trace_out.at[k],
            dst_ref=trace_in.at[k],
            send_sem=send_sem.at[6 * PER_STAGE + k],
            recv_sem=recv_sem.at[6 * PER_STAGE + k],
            device_id=at(0, shift),
            device_id_type=MESH,
        )
        for k, shift in enumerate((1, -1))
    ]

    def make_traces():
        for k in range(4, 7):
            loads[k].wait()
        for k in range(2):
            trace_out[k] = dot3(traces[k], state[...])

    def lift_blocks():
        loads[7].wait()
        head, tail = two_parts(lift[...])
        lift_parts[...] = jnp.zeros((96, 135), jnp.bfloat16)
        lift_parts[0:45, :] = head
        lift_parts[48:93, :] = tail
        factor = lift_parts[...]

        def lift_rows(k, carry):
            block(k).wait()
            for i in range(rows):
                both = mxu(factor, inverse[rows * k + i])
                lifted_blocks[rows * k + i] = both[:48] + both[48:]
            return carry

        lax.fori_loop(0, CHUNKS, lift_rows, 0)

    def make_rhs():
        for k in range(8, 12):
            loads[k].wait()
        for copy in spans:
            copy.wait_recv()
        position = lax.broadcasted_iota(jnp.int32, (256, 256), 0)
        total = residual[...]
        for k in range(2):
            edge = 0 if k == 0 else SPANS - 1
            arrived = trace_in[k] * jnp.where(row == edge, 0.0, 1.0)
            wanted = jnp.broadcast_to(halo[pl.ds(k, 1), :], (256, 256))
            pick = jnp.where(position == wanted, 1.0, 0.0).astype(jnp.bfloat16)
            head, tail = two_parts(arrived)
            total = total - dot3(couplings[k], mxu(head, pick) + mxu(tail, pick), ((0,), (0,)))
        rhs[...] = total

    def multiply_base():
        def base_row(i):
            return jnp.sum(inverse[i].astype(jnp.float32) * rhs[...], axis=0, keepdims=True)

        def base_eight(k, carry):
            first = pl.multiple_of(8 * k, 8)
            base[pl.ds(first, 8), :] = jnp.concatenate([base_row(first + i) for i in range(8)], axis=0)
            return carry

        lax.fori_loop(0, 16, base_eight, 0)
        base[128:135, :] = jnp.concatenate([base_row(128 + i) for i in range(7)], axis=0)

    @pl.when(early)
    def _():
        make_traces()
        lift_blocks()

    @pl.when(even)
    def _():
        pl.semaphore_wait(barrier, len(first_even) + 2)
        start(stage_copies(0, 0, sorted_rotor, stator))

    @pl.when(odd)
    def _():
        pl.semaphore_wait(barrier, len(every) + len(last_even) + 2)
        start(stage_copies(1, 0, sorted_rotor, stator))

    @pl.when(late)
    def _():
        load_rest()
        make_traces()

    for copy in spans:
        copy.start()

    @pl.when(odd)
    def _():
        for stage in (1, 2):
            if stage == 2:
                make_rhs()
            for group in (0, 1):
                digits = guest_digits if group == 0 else own_digits
                before = stage_copies(group, stage - 1, sorted_rotor, stator)
                if stage == 1:
                    rotor_ref, stator_ref = sorted_rotor, stator
                else:
                    rotor_ref, stator_ref = moving.at[2 * group], moving.at[2 * group + 1]
                to = 2 * group + (4 if stage == 2 else 0)
                moved, met = land(
                    group, stage - 1, before, digits, rotor_ref, stator_ref, moving.at[to], moving.at[to + 1]
                )
                prepare(group, stage, digits, moved, met)
                start(stage_copies(group, stage, moving.at[to], moving.at[to + 1]))

    @pl.when(late)
    def _():
        lift_blocks()

    @pl.when(even)
    def _():
        make_rhs()

    multiply_base()

    for k, ref in enumerate((sorted_rotor, stator)):
        terms, speed = side_terms(ref)
        for v in range(5):
            own_terms[k, pl.ds(9 * v, 9), :] = terms[v]
        own_speed[k] = speed

    for copy in spans:
        copy.wait_send()

    @pl.when(even)
    def _():
        for copy in stage_copies(0, 0, sorted_rotor, stator):
            copy.wait_send()

    @pl.when(odd)
    def _():
        for group, stage in ((1, 0), (0, 1), (1, 1), (0, 2), (1, 2)):
            to = 2 * group + (4 if stage == 2 else 0)
            for copy in stage_copies(group, stage, moving.at[to], moving.at[to + 1]):
                copy.wait_send()

    for group, mine in enumerate((even, odd)):

        @pl.when(mine)
        def _(group=group):
            arriving = stage_copies(group, 2, moving.at[6], moving.at[7])
            land(group, 2, arriving, own_digits, moving.at[6], moving.at[7], last_rotor, last_stator)

    for k, (left, right) in enumerate(((sorted_rotor, last_stator), (last_rotor, stator))):
        terms, speed = side_terms(last_stator if k == 0 else last_rotor)
        fastest = 0.5 * jnp.maximum(speed, own_speed[k])
        for v in range(5):
            part = pl.ds(9 * v, 9)
            face_terms[k, part, :] = (
                own_terms[k, part, :] + terms[v] - fastest * (right[part, :] - left[part, :])
            )
    head, tail = two_parts(face_terms[0])
    turn = one_hot[...]
    flux = mxu(head, turn) + mxu(tail, turn)
    rotor_flux[...] = flux
    terms_ref[:, 0:128] = -flux
    terms_ref[:, 128:256] = face_terms[1]


def finish_kernel(lifted_blocks, base, terms_ref, rotor_flux, update_hbm, flux_hbm, update, store_sem):
    store_flux = pltpu.make_async_copy(rotor_flux, flux_hbm.at[:, 0, :], store_sem.at[0])
    store_flux.start()
    terms = terms_ref[...]

    def finish(part):
        weighted = lifted_blocks[part, 0:45, :] * terms[None]
        update[part, :] = base[part, :] + jnp.sum(weighted, axis=1)

    def finish_eight(k, carry):
        finish(pl.ds(pl.multiple_of(8 * k, 8), 8))
        return carry

    stores = []
    for k, (start, stop) in enumerate(((0, 64), (64, 128), (128, 135))):
        if stop == 135:
            finish(pl.ds(start, 7))
        else:
            lax.fori_loop(start // 8, stop // 8, finish_eight, 0)
        part = pl.ds(start, stop - start)
        store = pltpu.make_async_copy(update.at[part], update_hbm.at[part, 0, :], store_sem.at[1 + k])
        store.start()
        stores.append(store)
    store_flux.wait()
    for store in stores:
        store.wait()


def shards(
    increment,
    partners,
    rotor_faces,
    stator_faces,
    solution,
    residual,
    inverse_blocks,
    halo_lists,
    lifting,
    traces,
    couplings,
):
    def vmem(*shape, dtype=jnp.float32):
        return pltpu.VMEM(shape, dtype)

    face = (90, 128)
    anywhere = pl.BlockSpec(memory_space=pltpu.HBM)
    held = pl.pallas_call(
        kernel,
        out_shape=(
            vmem(135, 48, 256),
            vmem(135, 256),
            vmem(45, 256),
            vmem(45, 128),
        ),
        in_specs=[anywhere] * 11,
        out_specs=[pl.BlockSpec(memory_space=pltpu.VMEM)] * 4,
        scratch_shapes=[
            vmem(1, 1, dtype=jnp.int32),
            vmem(1, 128, dtype=jnp.int32),
            vmem(*face),
            vmem(*face),
            vmem(135, 256),
            vmem(135, 256),
            vmem(135, 135, 256, dtype=jnp.bfloat16),
            vmem(2, 256, dtype=jnp.int32),
            vmem(45, 135),
            vmem(2, 45, 135),
            vmem(2, 45, 135),
            vmem(128, 128, dtype=jnp.bfloat16),
            vmem(*face),
            vmem(8, 128),
            vmem(8, 128),
            vmem(8, *face),
            vmem(*face),
            vmem(*face),
            vmem(12, *face),
            vmem(36, *face),
            vmem(2, 45, 256),
            vmem(2, 45, 256),
            vmem(96, 135, dtype=jnp.bfloat16),
            vmem(135, 256),
            vmem(2, 45, 128),
            vmem(2, 9, 128),
            vmem(2, 45, 128),
            pltpu.SemaphoreType.DMA((12,)),
            pltpu.SemaphoreType.DMA((CHUNKS,)),
            pltpu.SemaphoreType.DMA((6 * PER_STAGE + 2,)),
            pltpu.SemaphoreType.DMA((6 * PER_STAGE + 2,)),
        ],
        compiler_params=pltpu.CompilerParams(
            collective_id=0, has_side_effects=True, vmem_limit_bytes=KA
        ),
    )(
        increment.reshape(1, 1),
        partners,
        rotor_faces,
        stator_faces,
        solution,
        residual,
        inverse_blocks.reshape(135, 135, 256),
        halo_lists,
        lifting.T,
        traces.transpose(1, 0, 2),
        couplings.transpose(2, 0, 1),
    )
    return pl.pallas_call(
        finish_kernel,
        out_shape=(
            jax.ShapeDtypeStruct((135, 1, 256), jnp.float32),
            jax.ShapeDtypeStruct((45, 1, 128), jnp.float32),
        ),
        in_specs=[pl.BlockSpec(memory_space=pltpu.VMEM)] * 4,
        out_specs=(anywhere, anywhere),
        scratch_shapes=[vmem(135, 256), pltpu.SemaphoreType.DMA((4,))],
        compiler_params=pltpu.CompilerParams(vmem_limit_bytes=KB),
    )(*held)


def solution(mesh):
    placed = (
        P("span"),
        P("span", "circ"),
        P(None, "span", "circ"),
        P(None, "span", "circ"),
        P(None, "span", "circ"),
        P(None, "span", "circ"),
        P(None, None, "span", "circ"),
        P(None, "span", "circ"),
        P(),
        P(),
        P(),
    )
    return jax.shard_map(
        shards,
        mesh=mesh,
        in_specs=placed,
        out_specs=(P(None, "span", "circ"), P(None, "span", "circ")),
        check_vma=False,
    )
```

```python
import functools

import jax
import jax.numpy as jnp
from jax import lax
from jax.experimental import pallas as pl
from jax.experimental.pallas import tpu as pltpu
from jax.sharding import PartitionSpec as P

GAMMA = 1.4
VISCOSITY = 0.3
CIRC = 32
SPANS = 8
MESH = pl.DeviceIdType.MESH
STEPS = {"near": (1, -1, 2, -2), "middle": (4, -4), "far": (12, -12)}
KINDS = ("near", "middle", "far")
ORDERS = (("middle", "far", "near"), ("near", "middle", "far"))
STAY = 4
DIGITS = 6
PER_STAGE = 7
CHUNKS = 5
KA = 50 * 1024 * 1024
KB = 4 * 1024 * 1024


def two_parts(value):
    head = value.astype(jnp.bfloat16)
    return head, (value - head.astype(jnp.float32)).astype(jnp.bfloat16)


def mxu(left, right, dims=((1,), (0,))):
    return lax.dot_general(left, right, (dims, ((), ())), preferred_element_type=jnp.float32)


def dot3(left, right, dims=((1,), (0,))):
    left_head, left_tail = two_parts(left)
    right_head, right_tail = two_parts(right)
    small = mxu(left_head, right_tail, dims) + mxu(left_tail, right_head, dims)
    return mxu(left_head, right_head, dims) + small


def side_terms(ref):
    var = [ref[9 * v : 9 * v + 9, :] for v in range(5)]
    vel = var[1] / var[0]
    kinetic = 0.5 * (var[1] * var[1] + var[2] * var[2] + var[3] * var[3]) / var[0]
    pressure = (GAMMA - 1.0) * (var[4] - kinetic)
    flux = [var[1], var[1] * vel + pressure, var[2] * vel, var[3] * vel, (var[4] + pressure) * vel]
    terms = [
        0.5 * flux[v] - 0.5 * VISCOSITY * ref[45 + 9 * v : 54 + 9 * v, :] for v in range(5)
    ]
    return terms, jnp.abs(vel) + jnp.sqrt(GAMMA * pressure / var[0])


def kernel(
    inc_hbm, partners_hbm, rotor_hbm, stator_hbm, solution_hbm, residual_hbm, inverse_hbm, halo_hbm, lift_hbm,
    traces_hbm, couplings_hbm, lifted_blocks, base, terms_ref, rotor_flux,
    inc, partners, rotor, stator, state, residual, inverse, halo, lift, traces, couplings,
    one_hot, sorted_rotor, own_digits, guest_digits, moving, last_rotor, last_stator,
    slots_out, slots_in, trace_out, trace_in, lift_parts, rhs, own_terms, own_speed, face_terms,
    load_sem, block_sem, send_sem, recv_sem,
):
    me = lax.axis_index("circ")
    row = lax.axis_index("span")

    def at(circ_shift, span_shift=0):
        return (lax.rem(me + circ_shift + CIRC, CIRC), lax.rem(row + span_shift + SPANS, SPANS))

    even = lax.rem(row, 2) == 0
    odd = jnp.logical_not(even)
    first_even, last_even = STEPS[ORDERS[0][0]], STEPS[ORDERS[0][2]]
    every = STEPS["far"] + STEPS["middle"] + STEPS["near"]
    barrier = pltpu.get_barrier_semaphore()

    def greet(circ_shift, span_shift):
        pl.semaphore_signal(barrier, inc=1, device_id=at(circ_shift, span_shift), device_id_type=MESH)

    @pl.when(even)
    def _():
        for shift in last_even:
            greet(shift, 1)
        greet(0, 1)
        greet(0, -1)

    @pl.when(odd)
    def _():
        for shift in first_even:
            greet(shift, -1)
        for shift in every:
            greet(shift, 0)
        greet(0, -1)
        greet(0, 1)

    pairs = [
        (partners_hbm, partners),
        (inc_hbm, inc),
        (rotor_hbm.at[:, 0, :], rotor),
        (stator_hbm.at[:, 0, :], stator),
        (traces_hbm.at[:, 0, :], traces.at[0]),
        (traces_hbm.at[:, 1, :], traces.at[1]),
        (solution_hbm.at[:, 0, :], state),
        (lift_hbm, lift),
        (couplings_hbm.at[:, 0, :], couplings.at[0]),
        (couplings_hbm.at[:, 1, :], couplings.at[1]),
        (halo_hbm.at[:, 0, :], halo),
        (residual_hbm.at[:, 0, :], residual),
    ]
    loads = [pltpu.make_async_copy(src, dst, load_sem.at[k]) for k, (src, dst) in enumerate(pairs)]
    for load in loads[:4]:
        load.start()
    rows = 135 // CHUNKS

    def block(k):
        part = pl.ds(rows * k, rows)
        return pltpu.make_async_copy(inverse_hbm.at[part], inverse.at[part], block_sem.at[k])

    def load_rest():
        for load in loads[4:]:
            load.start()
        for k in range(CHUNKS):
            block(k).start()

    early = me < 11
    late = jnp.logical_not(early)

    @pl.when(early)
    def _():
        load_rest()

    loads[0].wait()
    loads[1].wait()
    increment = jnp.broadcast_to(inc[...], (1, 128))
    remainder = jnp.bitwise_and(increment, 127)
    whole = jnp.right_shift(increment, 7)
    lane = lax.broadcasted_iota(jnp.int32, (1, 128), 1)
    steps = whole + jnp.where(lane < remainder, 1, 0)
    near_digit = jnp.bitwise_and(steps + 1, 3) - 1
    quarter = jnp.bitwise_and(jnp.right_shift(steps - near_digit, 2), 7)

    def among(*values):
        hit = quarter == values[0]
        for value in values[1:]:
            hit = jnp.logical_or(hit, quarter == value)
        return jnp.where(hit, 1, 0)

    middle_digit = among(1, 4, 6) - among(2, 7)
    far_digit = among(2, 3, 4) - among(5, 6)

    own_digits[...] = jnp.zeros((8, 128), jnp.float32)
    for k, value in enumerate((near_digit, middle_digit, far_digit)):
        own_digits[k : k + 1, :] = value.astype(jnp.float32)

    def slot_copy(group, stage, k, device, source):
        index = (3 * group + stage) * PER_STAGE + k
        return pltpu.make_async_remote_copy(
            src_ref=source,
            dst_ref=guest_digits if k == DIGITS else slots_in.at[6 * (3 * group + stage) + k],
            send_sem=send_sem.at[index],
            recv_sem=recv_sem.at[index],
            device_id=device,
            device_id_type=MESH,
        )

    def stage_copies(group, stage, rotor_ref, stator_ref):
        change = 0 if group == 1 or stage == 1 else 1 if stage == 0 else -1
        out = 2 * (3 * group + stage)
        sources = [slots_out.at[out], slots_out.at[out + 1], rotor_ref, stator_ref]
        made = [
            slot_copy(group, stage, k, at(shift, change), sources[k])
            for k, shift in enumerate(STEPS[ORDERS[group][stage]])
        ]
        if change:
            made.append(slot_copy(group, stage, STAY, at(0, change), rotor_ref))
            made.append(slot_copy(group, stage, STAY + 1, at(0, change), stator_ref))
        if change == 1:
            made.append(slot_copy(group, stage, DIGITS, at(0, change), own_digits))
        return made

    def digit_of(group, stage, digits):
        kind = KINDS.index(ORDERS[group][stage])
        return jnp.broadcast_to(digits[kind : kind + 1, :], (90, 128))

    def prepare(group, stage, digits, rotor_now, stator_now):
        digit = digit_of(group, stage, digits)
        out = 2 * (3 * group + stage)
        slots_out[out] = jnp.where(digit == 1.0, rotor_now, stator_now)
        slots_out[out + 1] = jnp.where(digit == -1.0, rotor_now, stator_now)

    def start(copies):
        for copy in copies:
            copy.start()

    def land(group, stage, copies, digits, rotor_ref, stator_ref, rotor_to, stator_to):
        for copy in copies:
            copy.wait_recv()
        digit = digit_of(group, stage, digits)
        slot = 6 * (3 * group + stage)
        plus, minus = slots_in[slot], slots_in[slot + 1]
        if group == 0 and stage != 1:
            rotor_ref, stator_ref = slots_in.at[slot + STAY], slots_in.at[slot + STAY + 1]
        rotor_new = jnp.where(digit == 0.0, rotor_ref[...], jnp.where(digit == 1.0, plus, minus))
        stator_new = jnp.where(digit == 0.0, stator_ref[...], jnp.where(digit == 1.0, minus, plus))
        if ORDERS[group][stage] == "near":
            rotor_new = jnp.where(digit == 2.0, slots_in[slot + 2], rotor_new)
            stator_new = jnp.where(digit == 2.0, slots_in[slot + 3], stator_new)
        rotor_to[...] = rotor_new
        stator_to[...] = stator_new
        return rotor_new, stator_new

    slot = jnp.bitwise_and(partners[...] + remainder, 127)
    sublane = lax.broadcasted_iota(jnp.int32, (128, 128), 0)
    one_hot[...] = jnp.where(sublane == jnp.broadcast_to(slot, (128, 128)), 1.0, 0.0).astype(jnp.bfloat16)
    turn = one_hot[...]
    across = ((1,), (1,))
    loads[2].wait()
    faces = rotor[...]
    head, tail = two_parts(faces)
    rest = (faces - head.astype(jnp.float32) - tail.astype(jnp.float32)).astype(jnp.bfloat16)
    in_order = mxu(head, turn, across) + (mxu(tail, turn, across) + mxu(rest, turn, across))
    sorted_rotor[...] = in_order
    loads[3].wait()
    for group, mine in enumerate((even, odd)):

        @pl.when(mine)
        def _(group=group):
            prepare(group, 0, own_digits, sorted_rotor[...], stator[...])

    spans = [
        pltpu.make_async_remote_copy(
            src_ref=trace_out.at[k],
            dst_ref=trace_in.at[k],
            send_sem=send_sem.at[6 * PER_STAGE + k],
            recv_sem=recv_sem.at[6 * PER_STAGE + k],
            device_id=at(0, shift),
            device_id_type=MESH,
        )
        for k, shift in enumerate((1, -1))
    ]

    def make_traces():
        for k in range(4, 7):
            loads[k].wait()
        for k in range(2):
            trace_out[k] = dot3(traces[k], state[...])

    def lift_blocks():
        loads[7].wait()
        head, tail = two_parts(lift[...])
        lift_parts[...] = jnp.zeros((96, 135), jnp.bfloat16)
        lift_parts[0:45, :] = head
        lift_parts[48:93, :] = tail
        factor = lift_parts[...]

        def lift_rows(k, carry):
            block(k).wait()
            for i in range(rows):
                both = mxu(factor, inverse[rows * k + i])
                lifted_blocks[rows * k + i] = both[:48] + both[48:]
            return carry

        lax.fori_loop(0, CHUNKS, lift_rows, 0)

    def make_rhs():
        for k in range(8, 12):
            loads[k].wait()
        for copy in spans:
            copy.wait_recv()
        position = lax.broadcasted_iota(jnp.int32, (256, 256), 0)
        total = residual[...]
        for k in range(2):
            edge = 0 if k == 0 else SPANS - 1
            arrived = trace_in[k] * jnp.where(row == edge, 0.0, 1.0)
            wanted = jnp.broadcast_to(halo[pl.ds(k, 1), :], (256, 256))
            pick = jnp.where(position == wanted, 1.0, 0.0).astype(jnp.bfloat16)
            head, tail = two_parts(arrived)
            total = total - dot3(couplings[k], mxu(head, pick) + mxu(tail, pick), ((0,), (0,)))
        rhs[...] = total

    def multiply_base():
        def base_row(i):
            return jnp.sum(inverse[i].astype(jnp.float32) * rhs[...], axis=0, keepdims=True)

        def base_eight(k, carry):
            first = pl.multiple_of(8 * k, 8)
            base[pl.ds(first, 8), :] = jnp.concatenate([base_row(first + i) for i in range(8)], axis=0)
            return carry

        lax.fori_loop(0, 16, base_eight, 0)
        base[128:135, :] = jnp.concatenate([base_row(128 + i) for i in range(7)], axis=0)

    @pl.when(early)
    def _():
        make_traces()
        lift_blocks()

    @pl.when(even)
    def _():
        pl.semaphore_wait(barrier, len(first_even) + 2)
        start(stage_copies(0, 0, sorted_rotor, stator))

    @pl.when(odd)
    def _():
        pl.semaphore_wait(barrier, len(every) + len(last_even) + 2)
        start(stage_copies(1, 0, sorted_rotor, stator))

    @pl.when(late)
    def _():
        load_rest()
        make_traces()

    for copy in spans:
        copy.start()

    @pl.when(odd)
    def _():
        for stage in (1, 2):
            if stage == 2:
                make_rhs()
            for group in (0, 1):
                digits = guest_digits if group == 0 else own_digits
                before = stage_copies(group, stage - 1, sorted_rotor, stator)
                if stage == 1:
                    rotor_ref, stator_ref = sorted_rotor, stator
                else:
                    rotor_ref, stator_ref = moving.at[2 * group], moving.at[2 * group + 1]
                to = 2 * group + (4 if stage == 2 else 0)
                moved, met = land(
                    group, stage - 1, before, digits, rotor_ref, stator_ref, moving.at[to], moving.at[to + 1]
                )
                prepare(group, stage, digits, moved, met)
                start(stage_copies(group, stage, moving.at[to], moving.at[to + 1]))

    @pl.when(late)
    def _():
        lift_blocks()

    @pl.when(even)
    def _():
        make_rhs()

    multiply_base()

    for k, ref in enumerate((sorted_rotor, stator)):
        terms, speed = side_terms(ref)
        for v in range(5):
            own_terms[k, pl.ds(9 * v, 9), :] = terms[v]
        own_speed[k] = speed

    for copy in spans:
        copy.wait_send()

    @pl.when(even)
    def _():
        for copy in stage_copies(0, 0, sorted_rotor, stator):
            copy.wait_send()

    @pl.when(odd)
    def _():
        for group, stage in ((1, 0), (0, 1), (1, 1), (0, 2), (1, 2)):
            to = 2 * group + (4 if stage == 2 else 0)
            for copy in stage_copies(group, stage, moving.at[to], moving.at[to + 1]):
                copy.wait_send()

    for group, mine in enumerate((even, odd)):

        @pl.when(mine)
        def _(group=group):
            arriving = stage_copies(group, 2, moving.at[6], moving.at[7])
            land(group, 2, arriving, own_digits, moving.at[6], moving.at[7], last_rotor, last_stator)

    for k, (left, right) in enumerate(((sorted_rotor, last_stator), (last_rotor, stator))):
        terms, speed = side_terms(last_stator if k == 0 else last_rotor)
        fastest = 0.5 * jnp.maximum(speed, own_speed[k])
        for v in range(5):
            part = pl.ds(9 * v, 9)
            face_terms[k, part, :] = (
                own_terms[k, part, :] + terms[v] - fastest * (right[part, :] - left[part, :])
            )
    head, tail = two_parts(face_terms[0])
    turn = one_hot[...]
    flux = mxu(head, turn) + mxu(tail, turn)
    rotor_flux[...] = flux
    terms_ref[45:48, :] = jnp.zeros((3, 256), jnp.float32)
    terms_ref[0:45, 0:128] = -flux
    terms_ref[0:45, 128:256] = face_terms[1]


def finish_kernel(lifted_blocks, base, terms_ref, rotor_flux, update_hbm, flux_hbm, update, store_sem):
    store_flux = pltpu.make_async_copy(rotor_flux, flux_hbm.at[:, 0, :], store_sem.at[0])
    store_flux.start()
    terms = [terms_ref[8 * t : 8 * t + 8, :] for t in range(6)]
    sublane = lax.broadcasted_iota(jnp.int32, (8, 256), 0)
    lower = [jnp.bitwise_and(sublane, step) == 0 for step in (1, 2, 4)]

    def sum_sublanes(arrays):
        for k, mask in enumerate(lower):
            arrays = [
                jnp.where(mask, first, second) + pltpu.roll(jnp.where(mask, second, first), 1 << k, 0)
                for first, second in zip(arrays[0::2], arrays[1::2])
            ]
        return arrays[0]

    def row_tile(i):
        parts = [lifted_blocks[i, 8 * t : 8 * t + 8, :] * terms[t] for t in range(6)]
        return ((parts[0] + parts[1]) + (parts[2] + parts[3])) + (parts[4] + parts[5])

    def finish_eight(k, carry):
        first = pl.multiple_of(8 * k, 8)
        part = pl.ds(first, 8)
        update[part, :] = base[part, :] + sum_sublanes([row_tile(first + i) for i in range(8)])
        return carry

    def finish(part):
        rest = [row_tile(128 + i) for i in range(7)]
        update[part, :] = base[part, :] + sum_sublanes(rest + rest[:1])[0:7]

    stores = []
    for k, (start, stop) in enumerate(((0, 64), (64, 128), (128, 135))):
        if stop == 135:
            finish(pl.ds(start, 7))
        else:
            lax.fori_loop(start // 8, stop // 8, finish_eight, 0, unroll=4)
        part = pl.ds(start, stop - start)
        store = pltpu.make_async_copy(update.at[part], update_hbm.at[part, 0, :], store_sem.at[1 + k])
        store.start()
        stores.append(store)
    store_flux.wait()
    for store in stores:
        store.wait()


def shards(
    increment,
    partners,
    rotor_faces,
    stator_faces,
    solution,
    residual,
    inverse_blocks,
    halo_lists,
    lifting,
    traces,
    couplings,
):
    def vmem(*shape, dtype=jnp.float32):
        return pltpu.VMEM(shape, dtype)

    face = (90, 128)
    anywhere = pl.BlockSpec(memory_space=pltpu.HBM)
    held = pl.pallas_call(
        kernel,
        out_shape=(
            vmem(135, 48, 256),
            vmem(135, 256),
            vmem(48, 256),
            vmem(45, 128),
        ),
        in_specs=[anywhere] * 11,
        out_specs=[pl.BlockSpec(memory_space=pltpu.VMEM)] * 4,
        scratch_shapes=[
            vmem(1, 1, dtype=jnp.int32),
            vmem(1, 128, dtype=jnp.int32),
            vmem(*face),
            vmem(*face),
            vmem(135, 256),
            vmem(135, 256),
            vmem(135, 135, 256, dtype=jnp.bfloat16),
            vmem(2, 256, dtype=jnp.int32),
            vmem(45, 135),
            vmem(2, 45, 135),
            vmem(2, 45, 135),
            vmem(128, 128, dtype=jnp.bfloat16),
            vmem(*face),
            vmem(8, 128),
            vmem(8, 128),
            vmem(8, *face),
            vmem(*face),
            vmem(*face),
            vmem(12, *face),
            vmem(36, *face),
            vmem(2, 45, 256),
            vmem(2, 45, 256),
            vmem(96, 135, dtype=jnp.bfloat16),
            vmem(135, 256),
            vmem(2, 45, 128),
            vmem(2, 9, 128),
            vmem(2, 45, 128),
            pltpu.SemaphoreType.DMA((12,)),
            pltpu.SemaphoreType.DMA((CHUNKS,)),
            pltpu.SemaphoreType.DMA((6 * PER_STAGE + 2,)),
            pltpu.SemaphoreType.DMA((6 * PER_STAGE + 2,)),
        ],
        compiler_params=pltpu.CompilerParams(
            collective_id=0, has_side_effects=True, vmem_limit_bytes=KA
        ),
    )(
        increment.reshape(1, 1),
        partners,
        rotor_faces,
        stator_faces,
        solution,
        residual,
        inverse_blocks.reshape(135, 135, 256),
        halo_lists,
        lifting.T,
        traces.transpose(1, 0, 2),
        couplings.transpose(2, 0, 1),
    )
    return pl.pallas_call(
        finish_kernel,
        out_shape=(
            jax.ShapeDtypeStruct((135, 1, 256), jnp.float32),
            jax.ShapeDtypeStruct((45, 1, 128), jnp.float32),
        ),
        in_specs=[pl.BlockSpec(memory_space=pltpu.VMEM)] * 4,
        out_specs=(anywhere, anywhere),
        scratch_shapes=[vmem(135, 256), pltpu.SemaphoreType.DMA((4,))],
        compiler_params=pltpu.CompilerParams(vmem_limit_bytes=KB),
    )(*held)


def solution(mesh):
    placed = (
        P("span"),
        P("span", "circ"),
        P(None, "span", "circ"),
        P(None, "span", "circ"),
        P(None, "span", "circ"),
        P(None, "span", "circ"),
        P(None, None, "span", "circ"),
        P(None, "span", "circ"),
        P(),
        P(),
        P(),
    )
    return jax.shard_map(
        shards,
        mesh=mesh,
        in_specs=placed,
        out_specs=(P(None, "span", "circ"), P(None, "span", "circ")),
        check_vma=False,
    )
```

```python
import functools

import jax
import jax.numpy as jnp
from jax import lax
from jax.experimental import pallas as pl
from jax.experimental.pallas import tpu as pltpu
from jax.sharding import PartitionSpec as P

GAMMA = 1.4
VISCOSITY = 0.3
CIRC = 32
SPANS = 8
MESH = pl.DeviceIdType.MESH
STEPS = {"near": (1, -1, 2, -2), "middle": (4, -4), "far": (12, -12)}
KINDS = ("near", "middle", "far")
ORDERS = (("middle", "far", "near"), ("near", "middle", "far"))
STAY = 4
DIGITS = 6
PER_STAGE = 7
CHUNKS = 5
KA = 50 * 1024 * 1024
KB = 4 * 1024 * 1024


def two_parts(value):
    head = value.astype(jnp.bfloat16)
    return head, (value - head.astype(jnp.float32)).astype(jnp.bfloat16)


def mxu(left, right, dims=((1,), (0,))):
    return lax.dot_general(left, right, (dims, ((), ())), preferred_element_type=jnp.float32)


def dot3(left, right, dims=((1,), (0,))):
    left_head, left_tail = two_parts(left)
    right_head, right_tail = two_parts(right)
    small = mxu(left_head, right_tail, dims) + mxu(left_tail, right_head, dims)
    return mxu(left_head, right_head, dims) + small


def side_terms(ref):
    var = [ref[9 * v : 9 * v + 9, :] for v in range(5)]
    vel = var[1] / var[0]
    kinetic = 0.5 * (var[1] * var[1] + var[2] * var[2] + var[3] * var[3]) / var[0]
    pressure = (GAMMA - 1.0) * (var[4] - kinetic)
    flux = [var[1], var[1] * vel + pressure, var[2] * vel, var[3] * vel, (var[4] + pressure) * vel]
    terms = [
        0.5 * flux[v] - 0.5 * VISCOSITY * ref[45 + 9 * v : 54 + 9 * v, :] for v in range(5)
    ]
    return terms, jnp.abs(vel) + jnp.sqrt(GAMMA * pressure / var[0])


def kernel(
    inc_hbm, partners_hbm, rotor_hbm, stator_hbm, solution_hbm, residual_hbm, inverse_hbm, halo_hbm, lift_hbm,
    traces_hbm, couplings_hbm, lifted_blocks, base, terms_ref, rotor_flux,
    inc, partners, rotor, stator, state, residual, inverse, halo, lift, traces, couplings,
    one_hot, sorted_rotor, own_digits, guest_digits, moving, last_rotor, last_stator,
    slots_out, slots_in, trace_out, trace_in, lift_parts, rhs, own_terms, own_speed, face_terms,
    load_sem, block_sem, send_sem, recv_sem,
):
    me = lax.axis_index("circ")
    row = lax.axis_index("span")

    def at(circ_shift, span_shift=0):
        return (lax.rem(me + circ_shift + CIRC, CIRC), lax.rem(row + span_shift + SPANS, SPANS))

    even = lax.rem(row, 2) == 0
    odd = jnp.logical_not(even)
    first_even, last_even = STEPS[ORDERS[0][0]], STEPS[ORDERS[0][2]]
    every = STEPS["far"] + STEPS["middle"] + STEPS["near"]
    barrier = pltpu.get_barrier_semaphore()

    def greet(circ_shift, span_shift):
        pl.semaphore_signal(barrier, inc=1, device_id=at(circ_shift, span_shift), device_id_type=MESH)

    @pl.when(even)
    def _():
        for shift in last_even:
            greet(shift, 1)
        greet(0, 1)
        greet(0, -1)

    @pl.when(odd)
    def _():
        for shift in first_even:
            greet(shift, -1)
        for shift in every:
            greet(shift, 0)
        greet(0, -1)
        greet(0, 1)

    pairs = [
        (partners_hbm, partners),
        (inc_hbm, inc),
        (rotor_hbm.at[:, 0, :], rotor),
        (stator_hbm.at[:, 0, :], stator),
        (traces_hbm.at[:, 0, :], traces.at[0]),
        (traces_hbm.at[:, 1, :], traces.at[1]),
        (solution_hbm.at[:, 0, :], state),
        (lift_hbm, lift),
        (couplings_hbm.at[:, 0, :], couplings.at[0]),
        (couplings_hbm.at[:, 1, :], couplings.at[1]),
        (halo_hbm.at[:, 0, :], halo),
        (residual_hbm.at[:, 0, :], residual),
    ]
    loads = [pltpu.make_async_copy(src, dst, load_sem.at[k]) for k, (src, dst) in enumerate(pairs)]
    for load in loads[:4]:
        load.start()
    rows = 135 // CHUNKS

    def block(k):
        part = pl.ds(rows * k, rows)
        return pltpu.make_async_copy(inverse_hbm.at[part], inverse.at[part], block_sem.at[k])

    def load_rest():
        for load in loads[4:]:
            load.start()
        for k in range(CHUNKS):
            block(k).start()

    early = me < 10
    late = jnp.logical_not(early)

    @pl.when(early)
    def _():
        load_rest()

    loads[0].wait()
    loads[1].wait()
    increment = jnp.broadcast_to(inc[...], (1, 128))
    remainder = jnp.bitwise_and(increment, 127)
    whole = jnp.right_shift(increment, 7)
    lane = lax.broadcasted_iota(jnp.int32, (1, 128), 1)
    steps = whole + jnp.where(lane < remainder, 1, 0)
    near_digit = jnp.bitwise_and(steps + 1, 3) - 1
    quarter = jnp.bitwise_and(jnp.right_shift(steps - near_digit, 2), 7)

    def among(*values):
        hit = quarter == values[0]
        for value in values[1:]:
            hit = jnp.logical_or(hit, quarter == value)
        return jnp.where(hit, 1, 0)

    middle_digit = among(1, 4, 6) - among(2, 7)
    far_digit = among(2, 3, 4) - among(5, 6)

    own_digits[...] = jnp.zeros((8, 128), jnp.float32)
    for k, value in enumerate((near_digit, middle_digit, far_digit)):
        own_digits[k : k + 1, :] = value.astype(jnp.float32)

    def slot_copy(group, stage, k, device, source):
        index = (3 * group + stage) * PER_STAGE + k
        return pltpu.make_async_remote_copy(
            src_ref=source,
            dst_ref=guest_digits if k == DIGITS else slots_in.at[6 * (3 * group + stage) + k],
            send_sem=send_sem.at[index],
            recv_sem=recv_sem.at[index],
            device_id=device,
            device_id_type=MESH,
        )

    def stage_copies(group, stage, rotor_ref, stator_ref):
        change = 0 if group == 1 or stage == 1 else 1 if stage == 0 else -1
        out = 2 * (3 * group + stage)
        sources = [slots_out.at[out], slots_out.at[out + 1], rotor_ref, stator_ref]
        made = [
            slot_copy(group, stage, k, at(shift, change), sources[k])
            for k, shift in enumerate(STEPS[ORDERS[group][stage]])
        ]
        if change:
            made.append(slot_copy(group, stage, STAY, at(0, change), rotor_ref))
            made.append(slot_copy(group, stage, STAY + 1, at(0, change), stator_ref))
        if change == 1:
            made.append(slot_copy(group, stage, DIGITS, at(0, change), own_digits))
        return made

    def digit_of(group, stage, digits):
        kind = KINDS.index(ORDERS[group][stage])
        return jnp.broadcast_to(digits[kind : kind + 1, :], (90, 128))

    def prepare(group, stage, digits, rotor_now, stator_now):
        digit = digit_of(group, stage, digits)
        out = 2 * (3 * group + stage)
        slots_out[out] = jnp.where(digit == 1.0, rotor_now, stator_now)
        slots_out[out + 1] = jnp.where(digit == -1.0, rotor_now, stator_now)

    def start(copies):
        for copy in copies:
            copy.start()

    def land(group, stage, copies, digits, rotor_ref, stator_ref, rotor_to, stator_to):
        for copy in copies:
            copy.wait_recv()
        digit = digit_of(group, stage, digits)
        slot = 6 * (3 * group + stage)
        plus, minus = slots_in[slot], slots_in[slot + 1]
        if group == 0 and stage != 1:
            rotor_ref, stator_ref = slots_in.at[slot + STAY], slots_in.at[slot + STAY + 1]
        rotor_new = jnp.where(digit == 0.0, rotor_ref[...], jnp.where(digit == 1.0, plus, minus))
        stator_new = jnp.where(digit == 0.0, stator_ref[...], jnp.where(digit == 1.0, minus, plus))
        if ORDERS[group][stage] == "near":
            rotor_new = jnp.where(digit == 2.0, slots_in[slot + 2], rotor_new)
            stator_new = jnp.where(digit == 2.0, slots_in[slot + 3], stator_new)
        rotor_to[...] = rotor_new
        stator_to[...] = stator_new
        return rotor_new, stator_new

    slot = jnp.bitwise_and(partners[...] + remainder, 127)
    sublane = lax.broadcasted_iota(jnp.int32, (128, 128), 0)
    one_hot[...] = jnp.where(sublane == jnp.broadcast_to(slot, (128, 128)), 1.0, 0.0).astype(jnp.bfloat16)
    turn = one_hot[...]
    across = ((1,), (1,))
    loads[2].wait()
    faces = rotor[...]
    head, tail = two_parts(faces)
    rest = (faces - head.astype(jnp.float32) - tail.astype(jnp.float32)).astype(jnp.bfloat16)
    in_order = mxu(head, turn, across) + (mxu(tail, turn, across) + mxu(rest, turn, across))
    sorted_rotor[...] = in_order
    loads[3].wait()
    for group, mine in enumerate((even, odd)):

        @pl.when(mine)
        def _(group=group):
            prepare(group, 0, own_digits, sorted_rotor[...], stator[...])

    spans = [
        pltpu.make_async_remote_copy(
            src_ref=trace_out.at[k],
            dst_ref=trace_in.at[k],
            send_sem=send_sem.at[6 * PER_STAGE + k],
            recv_sem=recv_sem.at[6 * PER_STAGE + k],
            device_id=at(0, shift),
            device_id_type=MESH,
        )
        for k, shift in enumerate((1, -1))
    ]

    def make_traces():
        for k in range(4, 7):
            loads[k].wait()
        for k in range(2):
            trace_out[k] = dot3(traces[k], state[...])

    def lift_blocks():
        loads[7].wait()
        head, tail = two_parts(lift[...])
        lift_parts[...] = jnp.zeros((96, 135), jnp.bfloat16)
        lift_parts[0:45, :] = head
        lift_parts[48:93, :] = tail
        factor = lift_parts[...]

        def lift_rows(k, carry):
            block(k).wait()
            for i in range(rows):
                both = mxu(factor, inverse[rows * k + i])
                lifted_blocks[rows * k + i] = both[:48] + both[48:]
            return carry

        lax.fori_loop(0, CHUNKS, lift_rows, 0)

    def make_rhs():
        for k in range(8, 12):
            loads[k].wait()
        for copy in spans:
            copy.wait_recv()
        position = lax.broadcasted_iota(jnp.int32, (256, 256), 0)
        total = residual[...]
        for k in range(2):
            edge = 0 if k == 0 else SPANS - 1
            arrived = trace_in[k] * jnp.where(row == edge, 0.0, 1.0)
            wanted = jnp.broadcast_to(halo[pl.ds(k, 1), :], (256, 256))
            pick = jnp.where(position == wanted, 1.0, 0.0).astype(jnp.bfloat16)
            head, tail = two_parts(arrived)
            total = total - dot3(couplings[k], mxu(head, pick) + mxu(tail, pick), ((0,), (0,)))
        rhs[...] = total

    def multiply_base():
        def base_row(i):
            return jnp.sum(inverse[i].astype(jnp.float32) * rhs[...], axis=0, keepdims=True)

        def base_eight(k, carry):
            first = pl.multiple_of(8 * k, 8)
            base[pl.ds(first, 8), :] = jnp.concatenate([base_row(first + i) for i in range(8)], axis=0)
            return carry

        lax.fori_loop(0, 16, base_eight, 0)
        base[128:135, :] = jnp.concatenate([base_row(128 + i) for i in range(7)], axis=0)

    @pl.when(early)
    def _():
        make_traces()
        lift_blocks()

    @pl.when(even)
    def _():
        pl.semaphore_wait(barrier, len(first_even) + 2)
        start(stage_copies(0, 0, sorted_rotor, stator))

    @pl.when(odd)
    def _():
        pl.semaphore_wait(barrier, len(every) + len(last_even) + 2)
        start(stage_copies(1, 0, sorted_rotor, stator))

    @pl.when(late)
    def _():
        load_rest()
        make_traces()

    for copy in spans:
        copy.start()

    @pl.when(odd)
    def _():
        for stage in (1, 2):
            if stage == 2:
                make_rhs()
            for group in (0, 1):
                digits = guest_digits if group == 0 else own_digits
                before = stage_copies(group, stage - 1, sorted_rotor, stator)
                if stage == 1:
                    rotor_ref, stator_ref = sorted_rotor, stator
                else:
                    rotor_ref, stator_ref = moving.at[2 * group], moving.at[2 * group + 1]
                to = 2 * group + (4 if stage == 2 else 0)
                moved, met = land(
                    group, stage - 1, before, digits, rotor_ref, stator_ref, moving.at[to], moving.at[to + 1]
                )
                prepare(group, stage, digits, moved, met)
                start(stage_copies(group, stage, moving.at[to], moving.at[to + 1]))

    @pl.when(late)
    def _():
        lift_blocks()

    @pl.when(even)
    def _():
        make_rhs()

    multiply_base()

    for k, ref in enumerate((sorted_rotor, stator)):
        terms, speed = side_terms(ref)
        for v in range(5):
            own_terms[k, pl.ds(9 * v, 9), :] = terms[v]
        own_speed[k] = speed

    for copy in spans:
        copy.wait_send()

    @pl.when(even)
    def _():
        for copy in stage_copies(0, 0, sorted_rotor, stator):
            copy.wait_send()

    @pl.when(odd)
    def _():
        for group, stage in ((1, 0), (0, 1), (1, 1), (0, 2), (1, 2)):
            to = 2 * group + (4 if stage == 2 else 0)
            for copy in stage_copies(group, stage, moving.at[to], moving.at[to + 1]):
                copy.wait_send()

    for group, mine in enumerate((even, odd)):

        @pl.when(mine)
        def _(group=group):
            arriving = stage_copies(group, 2, moving.at[6], moving.at[7])
            land(group, 2, arriving, own_digits, moving.at[6], moving.at[7], last_rotor, last_stator)

    for k, (left, right) in enumerate(((sorted_rotor, last_stator), (last_rotor, stator))):
        terms, speed = side_terms(last_stator if k == 0 else last_rotor)
        fastest = 0.5 * jnp.maximum(speed, own_speed[k])
        for v in range(5):
            part = pl.ds(9 * v, 9)
            face_terms[k, part, :] = (
                own_terms[k, part, :] + terms[v] - fastest * (right[part, :] - left[part, :])
            )
    head, tail = two_parts(face_terms[0])
    turn = one_hot[...]
    flux = mxu(head, turn) + mxu(tail, turn)
    rotor_flux[...] = flux
    terms_ref[45:48, :] = jnp.zeros((3, 256), jnp.float32)
    terms_ref[0:45, 0:128] = -flux
    terms_ref[0:45, 128:256] = face_terms[1]


def finish_kernel(lifted_blocks, base, terms_ref, rotor_flux, update_hbm, flux_hbm, update, store_sem):
    store_flux = pltpu.make_async_copy(rotor_flux, flux_hbm.at[:, 0, :], store_sem.at[0])
    store_flux.start()
    terms = [terms_ref[8 * t : 8 * t + 8, :] for t in range(6)]
    sublane = lax.broadcasted_iota(jnp.int32, (8, 256), 0)
    lower = [jnp.bitwise_and(sublane, step) == 0 for step in (1, 2, 4)]

    def sum_sublanes(arrays):
        for k, mask in enumerate(lower):
            arrays = [
                jnp.where(mask, first, second) + pltpu.roll(jnp.where(mask, second, first), 1 << k, 0)
                for first, second in zip(arrays[0::2], arrays[1::2])
            ]
        return arrays[0]

    def row_tile(i):
        parts = [lifted_blocks[i, 8 * t : 8 * t + 8, :] * terms[t] for t in range(6)]
        return ((parts[0] + parts[1]) + (parts[2] + parts[3])) + (parts[4] + parts[5])

    def finish_eight(k, carry):
        first = pl.multiple_of(8 * k, 8)
        part = pl.ds(first, 8)
        update[part, :] = base[part, :] + sum_sublanes([row_tile(first + i) for i in range(8)])
        return carry

    def finish(part):
        rest = [row_tile(128 + i) for i in range(7)]
        update[part, :] = base[part, :] + sum_sublanes(rest + rest[:1])[0:7]

    stores = []
    for k, (start, stop) in enumerate(((0, 64), (64, 128), (128, 135))):
        if stop == 135:
            finish(pl.ds(start, 7))
        else:
            lax.fori_loop(start // 8, stop // 8, finish_eight, 0, unroll=8)
        part = pl.ds(start, stop - start)
        store = pltpu.make_async_copy(update.at[part], update_hbm.at[part, 0, :], store_sem.at[1 + k])
        store.start()
        stores.append(store)
    store_flux.wait()
    for store in stores:
        store.wait()


def shards(
    increment,
    partners,
    rotor_faces,
    stator_faces,
    solution,
    residual,
    inverse_blocks,
    halo_lists,
    lifting,
    traces,
    couplings,
):
    def vmem(*shape, dtype=jnp.float32):
        return pltpu.VMEM(shape, dtype)

    face = (90, 128)
    anywhere = pl.BlockSpec(memory_space=pltpu.HBM)
    held = pl.pallas_call(
        kernel,
        out_shape=(
            vmem(135, 48, 256),
            vmem(135, 256),
            vmem(48, 256),
            vmem(45, 128),
        ),
        in_specs=[anywhere] * 11,
        out_specs=[pl.BlockSpec(memory_space=pltpu.VMEM)] * 4,
        scratch_shapes=[
            vmem(1, 1, dtype=jnp.int32),
            vmem(1, 128, dtype=jnp.int32),
            vmem(*face),
            vmem(*face),
            vmem(135, 256),
            vmem(135, 256),
            vmem(135, 135, 256, dtype=jnp.bfloat16),
            vmem(2, 256, dtype=jnp.int32),
            vmem(45, 135),
            vmem(2, 45, 135),
            vmem(2, 45, 135),
            vmem(128, 128, dtype=jnp.bfloat16),
            vmem(*face),
            vmem(8, 128),
            vmem(8, 128),
            vmem(8, *face),
            vmem(*face),
            vmem(*face),
            vmem(12, *face),
            vmem(36, *face),
            vmem(2, 45, 256),
            vmem(2, 45, 256),
            vmem(96, 135, dtype=jnp.bfloat16),
            vmem(135, 256),
            vmem(2, 45, 128),
            vmem(2, 9, 128),
            vmem(2, 45, 128),
            pltpu.SemaphoreType.DMA((12,)),
            pltpu.SemaphoreType.DMA((CHUNKS,)),
            pltpu.SemaphoreType.DMA((6 * PER_STAGE + 2,)),
            pltpu.SemaphoreType.DMA((6 * PER_STAGE + 2,)),
        ],
        compiler_params=pltpu.CompilerParams(
            collective_id=0, has_side_effects=True, vmem_limit_bytes=KA
        ),
    )(
        increment.reshape(1, 1),
        partners,
        rotor_faces,
        stator_faces,
        solution,
        residual,
        inverse_blocks.reshape(135, 135, 256),
        halo_lists,
        lifting.T,
        traces.transpose(1, 0, 2),
        couplings.transpose(2, 0, 1),
    )
    return pl.pallas_call(
        finish_kernel,
        out_shape=(
            jax.ShapeDtypeStruct((135, 1, 256), jnp.float32),
            jax.ShapeDtypeStruct((45, 1, 128), jnp.float32),
        ),
        in_specs=[pl.BlockSpec(memory_space=pltpu.VMEM)] * 4,
        out_specs=(anywhere, anywhere),
        scratch_shapes=[vmem(135, 256), pltpu.SemaphoreType.DMA((4,))],
        compiler_params=pltpu.CompilerParams(vmem_limit_bytes=KB),
    )(*held)


def solution(mesh):
    placed = (
        P("span"),
        P("span", "circ"),
        P(None, "span", "circ"),
        P(None, "span", "circ"),
        P(None, "span", "circ"),
        P(None, "span", "circ"),
        P(None, None, "span", "circ"),
        P(None, "span", "circ"),
        P(),
        P(),
        P(),
    )
    return jax.shard_map(
        shards,
        mesh=mesh,
        in_specs=placed,
        out_specs=(P(None, "span", "circ"), P(None, "span", "circ")),
        check_vma=False,
    )
```
